256 devices in a mesh: seq: 64 (over y, z, core), mp: 4 (over x).
Axes of the slice: x: 4, y: 4, z: 8, core: 2. Of those that a mesh axis runs over, the one named last changes fastest.
Arguments:
- tile_batch: bfloat16 [256, 256, 1536], P('seq', None, 'mp'), may hold values from -6 to 6
- positions: int32 [256], P('seq'), may hold values from 0 to 8191, as said below
- counts: int32 [64], P('seq'), may hold values from 1 to 4, as said below
- vit_gain: float32 [1536], replicated, may hold values from 0.25 to 1.75
- vit_qkv: bfloat16 [1536, 3, 1536], P(None, None, 'mp')
- vit_out: bfloat16 [1536, 1536], P('mp'), may hold values from -0.15625 to 0.15625
- tile_proj: bfloat16 [1536, 768], replicated, may hold values from -0.15625 to 0.15625
- seq_cache: bfloat16 [8192, 768], P('seq'), may hold values from -6 to 6
- long_gain: float32 [768], replicated, may hold values from 0.25 to 1.75
- long_qkv: bfloat16 [768, 3, 768], P(None, None, 'mp')
- long_out: bfloat16 [768, 768], P('mp'), may hold values from -0.4375 to 0.4375
Outputs:
- longnet_out: bfloat16 [8192, 768], P('seq', 'mp')
The draws below stay inside these ranges and needn't reach their ends.
Inputs may be any that keep to these rules, and one draw needn't show every extreme that they name: The valid slots name distinct positions; all 256 slots name distinct positions. `counts`: some device holds exactly 4 tiles in every draw.
All inputs are finite; a program needn't handle non-finite values.
Results may differ from the reference program's by a relative error of at most 0.015.
Values may be sent and summed in bfloat16 or wider, within the bound.
No kernel may reach another device: no remote copies, remote signals or barrier semaphores. Data moves between devices by JAX's collectives and lax.ppermute only.
A program may use at most 128 MiB of HBM per device.

```python
import math
import jax
import jax.numpy as jnp
from jax import lax

HDT = 64
D_T = 1536
P_SIZE = 256
CAP = 4
HL = 16
HDL = 48
DL = 768
BRANCHES = 5
L = 8192
N_SEQ = 64


def draw_positions(key, part):
    shuffled = jax.random.permutation(key, L)
    return shuffled[:N_SEQ * CAP].astype(jnp.int32)


def draw_counts(key, part):
    first_key, second_key, third_key = jax.random.split(jax.random.fold_in(key, 11), 3)
    lower_draw = jax.random.randint(first_key, (N_SEQ,), 0, CAP)
    upper_draw = jax.random.randint(second_key, (N_SEQ,), 0, CAP)
    loads = 1 + lower_draw * upper_draw // (CAP - 1)
    busiest = jax.random.randint(third_key, (), 0, N_SEQ)
    return jnp.where(jnp.arange(N_SEQ) == busiest, CAP, loads).astype(jnp.int32)


def base_weights(key, width_in, width_out):
    base_key = jax.random.fold_in(key, 0)
    weights = jax.random.normal(base_key, (width_in, 3, width_out), jnp.float32) / math.sqrt(width_in)
    return weights


def draw_vit_qkv(key, part):
    key = jax.random.fold_in(key, 23)
    weights = base_weights(key, D_T, D_T)
    query_block = 4.0 * weights[:, 0]
    weights = jnp.stack([query_block, weights[:, 1], weights[:, 2]], axis=1)
    return weights.astype(jnp.bfloat16)


def draw_long_qkv(key, part):
    key = jax.random.fold_in(key, 29)
    weights = base_weights(key, DL, DL)
    return weights.astype(jnp.bfloat16)


def block_levels(key, dims, cuts, least, largest):
    def one(position, parts):
        steps = jax.random.uniform(jax.random.fold_in(jax.random.fold_in(key, 6), position), (parts,), jnp.float32, least / len(cuts), largest / len(cuts))
        return jnp.repeat(jnp.exp(steps), dims[position] // parts).reshape((-1,) + (1,) * (len(dims) - position - 1))

    level = one(*cuts[0])
    for cut in cuts[1:]:
        level = level * one(*cut)
    return level


def centred(stream_key, extent, scale, most, pieces=(), kind=jnp.bfloat16):
    factor_of = block_levels(stream_key, extent, pieces, -0.22, 0.18) if pieces else 1.0
    drawn = jax.random.normal(stream_key, extent, jnp.float32) * scale * factor_of
    return jnp.minimum(jnp.maximum(drawn, -most), most).astype(kind)


def setup_inputs(seed: int = 0) -> dict:
    arg_keys = jax.random.split(jax.random.key(seed), 12)
    return {
        "tile_batch": centred(arg_keys[0], (N_SEQ * CAP, P_SIZE, D_T), 1.0, 6.0, ((0, 64), (2, 4))),
        "positions": draw_positions(jax.random.fold_in(arg_keys[11], 71), 0),
        "counts": draw_counts(jax.random.fold_in(arg_keys[11], 71), 0),
        "vit_gain": jnp.clip(1.0 + 0.15 * jax.random.normal(arg_keys[3], (D_T,), jnp.float32), 0.25, 1.75),
        "vit_qkv": draw_vit_qkv(jax.random.fold_in(arg_keys[11], 71), 0),
        "vit_out": centred(arg_keys[5], (D_T, D_T), D_T ** -0.5, 0.15625, ((0, 4),)),
        "tile_proj": centred(arg_keys[6], (D_T, DL), D_T ** -0.5, 0.15625),
        "seq_cache": centred(arg_keys[7], (L, DL), 1.0, 6.0, ((0, 64),)),
        "long_gain": jnp.clip(1.0 + 0.15 * jax.random.normal(arg_keys[8], (DL,), jnp.float32), 0.25, 1.75),
        "long_qkv": draw_long_qkv(jax.random.fold_in(arg_keys[11], 71), 0),
        "long_out": centred(arg_keys[10], (DL, DL), (DL // 4) ** -0.5, 0.4375, ((0, 4),)),
    }


EPSILON = 1e-05
FLOOR_SCORE = -1e+30

def layer_norm(values, gain_row):
    widened = values.astype(jnp.float32)
    centre = widened - lax.optimization_barrier(jnp.mean(widened, axis=-1, keepdims=True))
    spread = lax.optimization_barrier(jnp.mean(centre * centre, axis=-1, keepdims=True))
    return (centre * lax.rsqrt(spread + EPSILON) * gain_row).astype(jnp.bfloat16)

def pool_tile(tile_rows, vit_gain, vit_qkv, vit_out):
    col_width = vit_qkv.shape[-1]
    head_count = col_width // HDT
    normed = layer_norm(tile_rows, vit_gain)
    projected = jnp.dot(normed, vit_qkv.reshape(vit_qkv.shape[0], 3 * col_width), preferred_element_type=jnp.float32)
    projected = projected.astype(jnp.bfloat16).reshape(tile_rows.shape[0], 3, head_count, HDT).astype(jnp.float32)
    scores = jnp.einsum('qhe,khe->hqk', projected[:, 0], projected[:, 1]) * HDT ** (-0.5)
    peak_score = lax.optimization_barrier(jnp.max(scores, axis=-1, keepdims=True))
    weights = jnp.exp(scores - peak_score)
    normalized = (weights / lax.optimization_barrier(jnp.sum(weights, axis=-1, keepdims=True))).astype(jnp.bfloat16).astype(jnp.float32)
    mixed_rows = jnp.einsum('hqk,khe->qhe', normalized, projected[:, 2]).astype(jnp.bfloat16)
    pooled = lax.optimization_barrier(jnp.mean(mixed_rows.astype(jnp.float32), axis=0)).reshape(1, col_width).astype(jnp.bfloat16)
    partial_value = jnp.dot(pooled, vit_out, preferred_element_type=jnp.float32)[0]
    return partial_value + lax.optimization_barrier(jnp.mean(tile_rows.astype(jnp.float32), axis=0))

def pick_rows(values, select):
    stride, head_count = select.shape
    shaped = values.reshape((values.shape[0] // stride, stride, head_count) + values.shape[2:])
    chosen = select.reshape((1, stride, head_count) + (1,) * (values.ndim - 2))
    return lax.optimization_barrier(jnp.sum(jnp.where(chosen, shaped, jnp.zeros((), values.dtype)), axis=1))

def spread_rows(values, select, fill_value):
    moved = jnp.moveaxis(values, 0, 1)
    stride = select.shape[0]
    tail_dims = moved.shape[2:]
    chosen = select.reshape((1,) + select.shape + (1,) * len(tail_dims))
    placed = jnp.where(chosen, moved[:, None], fill_value)
    return placed.reshape((moved.shape[0] * stride,) + moved.shape[1:])

def attend_segment(operands):
    q_rows, k_rows, v_rows = operands
    scores = jnp.einsum('qhe,khe->hqk', q_rows.astype(jnp.float32), k_rows.astype(jnp.float32)) * HDL ** (-0.5)
    highest = lax.optimization_barrier(jnp.max(scores, axis=-1))
    weights = jnp.exp(scores - highest[..., None])
    totals = lax.optimization_barrier(jnp.sum(weights, axis=-1))
    rounded = weights.astype(jnp.bfloat16).astype(jnp.float32)
    weighted = jnp.einsum('hqk,khe->hqe', rounded, v_rows.astype(jnp.float32))
    return (highest, totals, weighted)

def reference(tile_batch, positions, counts, vit_gain, vit_qkv, vit_out, tile_proj, seq_cache, long_gain, long_qkv, long_out):
    slot_count = tile_batch.shape[0]
    valid = jnp.arange(slot_count) % CAP < jnp.repeat(counts, CAP)

    def encode_one(operands):
        tile_rows, live = operands
        return lax.cond(live, lambda rows_in: pool_tile(rows_in, vit_gain, vit_qkv, vit_out), lambda rows_in: jnp.zeros((rows_in.shape[1],), jnp.float32), tile_rows)
    pooled = lax.map(encode_one, (tile_batch, valid))
    embeds = jnp.dot(pooled.astype(jnp.bfloat16), tile_proj, preferred_element_type=jnp.float32).astype(jnp.bfloat16)
    target = jnp.where(valid, positions, L).astype(jnp.int32)
    sequence = seq_cache.at[target].set(embeds, mode='drop')
    seq_norm = layer_norm(sequence, long_gain)
    projected = jnp.dot(seq_norm, long_qkv.reshape(DL, 3 * DL), preferred_element_type=jnp.float32)
    projected = projected.astype(jnp.bfloat16).reshape(L, 3, HL, HDL)
    queries, key_rows, values = (projected[:, 0], projected[:, 1], projected[:, 2])
    branch_peaks = []
    branch_totals = []
    branch_outs = []
    for level in range(BRANCHES):
        stride = 2 ** level
        span = L // 2 ** (BRANCHES - 1 - level)
        seg_count = L // span
        per_seg = span // stride
        select = jnp.arange(stride)[:, None] == (jnp.arange(HL) % stride)[None, :]
        q_pick = pick_rows(queries, select).reshape(seg_count, per_seg, HL, HDL)
        k_pick = pick_rows(key_rows, select).reshape(seg_count, per_seg, HL, HDL)
        v_pick = pick_rows(values, select).reshape(seg_count, per_seg, HL, HDL)
        highest, totals, weighted = lax.map(attend_segment, (q_pick, k_pick, v_pick))
        highest = jnp.moveaxis(highest, 0, 1).reshape(HL, L // stride)
        totals = jnp.moveaxis(totals, 0, 1).reshape(HL, L // stride)
        weighted = jnp.moveaxis(weighted, 0, 1).reshape(HL, L // stride, HDL)
        branch_peaks.append(spread_rows(highest, select, FLOOR_SCORE))
        branch_totals.append(spread_rows(totals, select, 0.0))
        branch_outs.append(spread_rows(weighted, select, 0.0))
    overall = branch_peaks[0]
    for level in range(1, BRANCHES):
        overall = jnp.maximum(overall, branch_peaks[level])
    numer = jnp.zeros((L, HL, HDL), jnp.float32)
    denom = jnp.zeros((L, HL), jnp.float32)
    for level in range(BRANCHES):
        factor = jnp.exp(branch_peaks[level] - overall)
        numer = numer + factor[..., None] * branch_outs[level]
        denom = denom + factor * branch_totals[level]
    attended = (numer / denom[..., None]).astype(jnp.bfloat16).reshape(L, DL)
    return jnp.dot(attended, long_out, preferred_element_type=jnp.float32).astype(jnp.bfloat16)
```

```python
import functools
import math

import jax
import jax.numpy as jnp
from jax import lax
from jax.experimental import pallas as pl
from jax.experimental.pallas import tpu as pltpu
from jax.sharding import PartitionSpec as P

HDT = 64
HDL = 48
BRANCHES = 5
EPSILON = 1e-05
FLOOR_SCORE = -1e30
BF = jnp.bfloat16
F32 = jnp.float32
ROWS = 128
BASES = (0, 256, 512, 768, 1024)


def params(mib=40):
    return pltpu.CompilerParams(vmem_limit_bytes=mib * 2**20)


def whole(kind=pltpu.VMEM):
    return pl.BlockSpec(memory_space=kind)


def dot(a, b):
    return jnp.dot(a, b, preferred_element_type=F32)


def dot_t(a, b):
    return lax.dot_general(a, b, (((1,), (1,)), ((), ())), preferred_element_type=F32)


def iota(shape, dim):
    return lax.broadcasted_iota(jnp.int32, shape, dim)


def encode_kernel(idx, own, left, right, far_a, far_b, gain, weight, out, xn, qk):
    mp = idx[0]
    tokens, width = own.shape[1], own.shape[2]
    features = 4 * width
    blocks = [lax.rem(mp + shift, 4) for shift in (0, 3, 1, 2)]
    starts = [pl.multiple_of(block * width, 128) for block in blocks]
    for t in range(2):
        far = far_a if t == 0 else far_b
        parts = [own[t], left[t], right[t], far[0]]
        wide = [part.astype(F32) for part in parts]
        total = sum(jnp.sum(part, axis=-1, keepdims=True) for part in wide)
        mean = total * (1.0 / features)
        centred = [part - mean for part in wide]
        spread = sum(jnp.sum(part * part, axis=-1, keepdims=True) for part in centred)
        scale = lax.rsqrt(spread * (1.0 / features) + EPSILON)
        for d in range(4):
            xn[d, t * tokens : (t + 1) * tokens, :] = (
                centred[d] * scale * gain[pl.ds(blocks[d], 1), 0, :]
            ).astype(BF)
        out[t : t + 1, width : 2 * width] = jnp.sum(wide[0], axis=0, keepdims=True) * (1.0 / tokens)
    acc = dot(xn[0], weight[pl.ds(starts[0], width), 0 : 2 * width])
    for d in range(1, 4):
        acc = acc + dot(xn[d], weight[pl.ds(starts[d], width), 0 : 2 * width])
    qk[...] = acc.astype(BF)
    lane = iota((tokens, 2 * HDT), 1)
    pooled = [[] for _ in range(4)]
    for t in range(2):
        low, high = t * tokens, (t + 1) * tokens
        rows = []
        for pair in range(width // (2 * HDT)):
            q2 = qk[low:high, pair * 128 : (pair + 1) * 128]
            k2 = qk[low:high, width + pair * 128 : width + (pair + 1) * 128]
            for half in range(2):
                qm = jnp.where((lane >= HDT) == (half == 1), q2, jnp.zeros((), BF))
                s = dot_t(qm, k2) * HDT ** (-0.5)
                e = jnp.exp(s - jnp.max(s, axis=-1, keepdims=True))
                share = 1.0 / (jnp.sum(e, axis=-1, keepdims=True) * tokens)
                rows.append(jnp.sum(e * share, axis=0, keepdims=True))
        rows.append(jnp.zeros((8 - len(rows), tokens), F32))
        mix = jnp.concatenate(rows, axis=0).astype(BF)
        for d in range(4):
            pooled[d].append(dot(mix, xn[d, low:high, :]))
    acc = jnp.zeros((16, width), F32)
    for d in range(4):
        acc = acc + dot(
            jnp.concatenate(pooled[d], axis=0).astype(BF),
            weight[pl.ds(starts[d], width), 2 * width : 3 * width],
        )
    keep = (iota((16, width), 0) & 7) == (iota((16, width), 1) >> 6)
    acc = jnp.where(keep, acc, 0.0)
    for t in range(2):
        out[t : t + 1, 0:width] = jnp.sum(acc[t * 8 : (t + 1) * 8], axis=0, keepdims=True)


def encode(idx, own, left, right, far_a, far_b, gain, weight):
    tokens, width = own.shape[1], own.shape[2]
    return pl.pallas_call(
        encode_kernel,
        out_shape=jax.ShapeDtypeStruct((2, 2 * width), F32),
        in_specs=[whole(pltpu.SMEM)] + [whole()] * 7,
        out_specs=whole(),
        scratch_shapes=[
            pltpu.VMEM((4, 2 * tokens, width), BF),
            pltpu.VMEM((2 * tokens, 2 * width), BF),
        ],
        compiler_params=params(),
        cost_estimate=pl.CostEstimate(
            flops=6 * 10**9, bytes_accessed=8 * 10**6, transcendentals=8 * 10**5
        ),
        name="encode",
    )(idx, own, left, right, far_a, far_b, gain, weight)


def norm_rows(x, gain):
    mean = jnp.mean(x, axis=-1, keepdims=True)
    centre = x - mean
    spread = jnp.mean(centre * centre, axis=-1, keepdims=True)
    return (centre * lax.rsqrt(spread + EPSILON) * gain).astype(BF)


def embed_kernel(a, b, c, d, tail, gain, weight, out):
    width = weight.shape[1]
    total = (a[...] + b[...]) + (c[...] + d[...])
    normed = norm_rows(total.astype(BF).astype(F32), gain[...])
    out[:, 0:width] = dot(normed, weight[...]).astype(BF)
    out[:, width:] = tail[...]


def embed_rows(parts, tail, gain, weight):
    rows, width = parts[0].shape[0], weight.shape[1]
    return pl.pallas_call(
        embed_kernel,
        out_shape=jax.ShapeDtypeStruct((rows, width + tail.shape[1]), BF),
        in_specs=[whole()] * 7,
        out_specs=whole(),
        compiler_params=params(),
        name="embed_rows",
    )(*parts, tail, gain, weight)


def rev4(x):
    return ((x & 1) << 3) | ((x & 2) << 1) | ((x & 4) >> 1) | ((x & 8) >> 3)


def pick_start(head, level):
    return pl.multiple_of((rev4(head & 15) >> (4 - level)) * (ROWS >> level), 8)


def local_row(j, level, head):
    bits = j >> 3
    free = 4 - level
    turned = rev4(bits) >> (4 - free) if free else bits * 0
    return (j & 7) * 16 + (turned << level) + (head & ((1 << level) - 1))


def slide_kernel(idx, cache, gain, weight, tail, q_out, picks, kv):
    heads_width = q_out.shape[1]
    first_head = idx[0] * 4
    row = iota((ROWS, ROWS), 0)
    turn = (local_row(row, 0, 0) == iota((ROWS, ROWS), 1)).astype(BF)
    normed = norm_rows(cache[...].astype(F32), gain[...])
    normed = dot(turn, normed).astype(BF)
    qkv = dot(normed, weight[...]).astype(BF).astype(F32)
    q_out[...] = qkv[:, 2 * heads_width :]
    kv[...] = qkv[:, : 2 * heads_width]
    base = 0
    for level in range(BRANCHES):
        n = ROWS >> level
        column = iota((n, 2 * heads_width), 1)
        column = jnp.where(column >= heads_width, column - heads_width, column)
        got = jnp.zeros((n, 2 * heads_width), F32)
        for h in range(4):
            here = (column >= h * HDL) & (column < (h + 1) * HDL)
            got = jnp.where(here, kv[pl.ds(pick_start(first_head + h, level), n), :], got)
        if level == BRANCHES - 1:
            got = jnp.concatenate([got, tail[...]], axis=0)
        picks[base : base + got.shape[0], :] = got.astype(BF)
        base += n


def slide_project(idx, cache, gain, weight, tail):
    hw = weight.shape[1] // 3
    return pl.pallas_call(
        slide_kernel,
        out_shape=(
            jax.ShapeDtypeStruct((ROWS, hw), F32),
            jax.ShapeDtypeStruct((2 * ROWS, 2 * hw), BF),
        ),
        in_specs=[whole(pltpu.SMEM)] + [whole()] * 4,
        out_specs=(whole(), whole()),
        scratch_shapes=[pltpu.VMEM((ROWS, 2 * hw), F32)],
        compiler_params=params(),
        name="slide_project",
    )(idx, cache, gain, weight, tail)


def key_rows(level):
    return 512 if level == BRANCHES - 1 else 256


def flag_kernel(idx, pos, out):
    first_head, seq = idx[0] * 4, idx[1]
    slots = pos.shape[0]
    for level in range(BRANCHES):
        half = key_rows(level)
        n = 16 if level == BRANCHES - 1 else ROWS >> level
        shift = n.bit_length() - 1
        k = iota((8, 2 * half), 1)
        in_half = k & (half - 1)
        source = seq ^ (2 * (in_half >> shift) + (k >= half).astype(jnp.int32))
        j = in_half & (n - 1)
        dead = (j >= 8) if level == BRANCHES - 1 else (j < 0)
        for h in range(4):
            if level == 0 and h > 0:
                out[h : h + 1, 0 : 2 * half] = out[0:1, 0 : 2 * half]
                continue
            place = source * ROWS + local_row(j & 7 if n == 16 else j, level, first_head + h)
            hit = jnp.max(
                (pos[...] == place[0:1]).astype(jnp.int32), axis=0, keepdims=True
            )
            gone = (hit > 0) | dead[0:1]
            r = level * 8 + h
            out[r : r + 1, 0 : 2 * half] = jnp.where(gone, FLOOR_SCORE, 0.0)


def key_flags(idx, pos):
    return pl.pallas_call(
        flag_kernel,
        out_shape=jax.ShapeDtypeStruct((8 * BRANCHES, 1024), F32),
        in_specs=[whole(pltpu.SMEM), whole()],
        out_specs=whole(),
        compiler_params=params(),
        name="key_flags",
    )(idx, pos)


def depth_of(x):
    return sum(((x & mask) == 0).astype(jnp.int32) for mask in (1, 3, 7, 15))


def attend_kernel(idx, q_cache, mine, theirs, bias, emb, out_w, o0, o1, o2, o3, q, peak, total, acc):
    mp, seq = idx[0], idx[1]
    first_head = mp * 4
    hw = q_cache.shape[1]
    scale = HDL ** (-0.5)
    slots = emb.shape[0]
    tail = emb[:, 3 * hw :]
    col = iota((8, tail.shape[1]), 1)
    digits = jnp.where(col == 0, 64.0, jnp.where(col == 1, 1.0, 0.0)).astype(BF)
    pos = dot_t(digits, tail).astype(jnp.int32)[0:1]
    own = seq * ROWS + local_row(iota((ROWS, 1), 0), 0, 0)
    match = own == pos
    found = jnp.max(match.astype(jnp.int32), axis=1, keepdims=True) > 0
    placed = dot(match.astype(BF), emb[:, 2 * hw : 3 * hw])
    q[...] = jnp.where(found, placed, q_cache[...])

    def head_mask(n, h):
        column = iota((n, hw), 1)
        return (column >= h * HDL) & (column < (h + 1) * HDL)

    def queries(level):
        n = ROWS >> level
        got = []
        for h in range(4):
            rows = q[...] if level == 0 else q[pl.ds(pick_start(first_head + h, level), n), :]
            got.append(jnp.where(head_mask(n, h), rows, 0.0))
        return jnp.concatenate(got, axis=0).astype(BF)

    full_q = queries(0)
    s = dot_t(full_q, emb[:, 0:hw]) * scale
    cross = (pos ^ (seq * ROWS)) >> 9
    first = sum(((cross >> b) != 0).astype(jnp.int32) for b in range(4))
    times = []
    for h in range(4):
        q_depth = depth_of(own ^ (first_head + h))
        k_depth = jnp.where(pos < 0, -1, depth_of(pos ^ (first_head + h)) - first)
        times.append(jnp.maximum(jnp.minimum(k_depth, q_depth - first) + 1, 0))
    times = jnp.concatenate(times, axis=0).astype(F32)
    s = jnp.where(times > 0.0, s, FLOOR_SCORE)
    m = jnp.max(s, axis=-1, keepdims=True)
    e = times * jnp.exp(s - m)
    peak[...] = jnp.broadcast_to(m, peak.shape)
    total[...] = jnp.broadcast_to(jnp.sum(e, axis=-1, keepdims=True), total.shape)
    acc[...] = dot(e.astype(BF), emb[:, hw : 2 * hw])

    for level in range(BRANCHES):
        n = ROWS >> level
        half = key_rows(level)
        low = BASES[level]
        qb = full_q if level == 0 else queries(level)
        sides = []
        for number, side in enumerate((mine, theirs)):
            s = dot_t(qb, side[low : low + half, 0:hw]) * scale
            flags = bias[level * 8 : level * 8 + 4, number * half : (number + 1) * half]
            s = s.reshape(4, n, half) + flags[:, None, :]
            sides.append(s.reshape(4 * n, half))
        m = jnp.maximum(
            jnp.max(sides[0], axis=-1, keepdims=True), jnp.max(sides[1], axis=-1, keepdims=True)
        )
        e0, e1 = jnp.exp(sides[0] - m), jnp.exp(sides[1] - m)
        t = jnp.sum(e0, axis=-1, keepdims=True) + jnp.sum(e1, axis=-1, keepdims=True)
        o = dot(e0.astype(BF), mine[low : low + half, hw : 2 * hw]) + dot(
            e1.astype(BF), theirs[low : low + half, hw : 2 * hw]
        )
        for h in range(4):
            start = h * ROWS + (0 if level == 0 else pick_start(first_head + h, level))
            at = pl.ds(pl.multiple_of(start, 8), n)
            part = slice(h * n, (h + 1) * n)
            before = peak[at, :]
            after = jnp.maximum(before, m[part])
            keep, add = jnp.exp(before - after), jnp.exp(m[part] - after)
            peak[at, :] = after
            total[at, :] = total[at, :] * keep + t[part] * add
            acc[at, :] = acc[at, :] * keep[:, 0:1] + o[part] * add[:, 0:1]

    attended = jnp.zeros((ROWS, hw), F32)
    for h in range(4):
        rows = slice(h * ROWS, (h + 1) * ROWS)
        attended = jnp.where(head_mask(ROWS, h), acc[rows, :] / total[rows, 0:1], attended)
    turn = (local_row(iota((ROWS, ROWS), 1), 0, 0) == iota((ROWS, ROWS), 0)).astype(BF)
    attended = dot(turn, attended.astype(BF)).astype(BF)
    for d, o in enumerate((o0, o1, o2, o3)):
        o[...] = dot(attended, out_w[lax.rem(mp + d, 4)]).astype(BF)


def attend(idx, q_cache, mine, theirs, bias, emb, out_w):
    hw = q_cache.shape[1]
    return pl.pallas_call(
        attend_kernel,
        out_shape=(jax.ShapeDtypeStruct((ROWS, hw), BF),) * 4,
        in_specs=[whole(pltpu.SMEM)] + [whole()] * 6,
        out_specs=(whole(),) * 4,
        scratch_shapes=[
            pltpu.VMEM((ROWS, hw), F32),
            pltpu.VMEM((4 * ROWS, 128), F32),
            pltpu.VMEM((4 * ROWS, 128), F32),
            pltpu.VMEM((4 * ROWS, hw), F32),
        ],
        compiler_params=params(),
        name="attend",
    )(idx, q_cache, mine, theirs, bias, emb, out_w)


def combine_kernel(a, b, c, d, out):
    out[...] = ((a[...].astype(F32) + b[...]) + (c[...].astype(F32) + d[...])).astype(BF)


def shift_mp(x, k):
    return lax.ppermute(x, "mp", [(i, (i + k) % 4) for i in range(4)])


def swap_seq(x, bit):
    return lax.ppermute(x, "seq", [(i, i ^ bit) for i in range(64)])


def local(
    tile_batch,
    positions,
    counts,
    vit_gain,
    vit_qkv,
    vit_out,
    tile_proj,
    seq_cache,
    long_gain,
    long_qkv,
    long_out,
):
    mp, seq = lax.axis_index("mp"), lax.axis_index("seq")
    idx = jnp.stack([mp, seq]).astype(jnp.int32)
    slots, _, width = tile_batch.shape
    model = seq_cache.shape[1]
    hw = long_qkv.shape[-1]

    chunks = [tile_batch[0:2], tile_batch[2:4]]
    near = [(shift_mp(chunk, 1), shift_mp(chunk, 3)) for chunk in chunks]
    far = [(shift_mp(a[0:1], 1), shift_mp(b[1:2], 3)) for a, b in near]

    sent = jnp.where(jnp.arange(slots) < counts[0], positions, -64)
    high, low = (sent >> 6).astype(F32), (sent & 63).astype(F32)

    slide_w = jnp.concatenate([long_qkv[:, 1], long_qkv[:, 2], long_qkv[:, 0]], axis=1)
    tail_row = jnp.zeros((8, 2 * hw), F32).at[0, 0:8].set(jnp.concatenate([high, low]))
    gain_row = long_gain.reshape(1, model)
    q_cache, picks = slide_project(idx, seq_cache, gain_row, slide_w, tail_row)
    have = picks[None]
    kept = []
    for level, bit in enumerate((2, 4, 8, 16, 32)):
        have = jnp.concatenate([have, swap_seq(have, bit)], axis=0)
        n = ROWS >> level
        if level < BRANCHES - 1:
            kept.append(have[:, 0:n].reshape(-1, 2 * hw))
            have = have[:, n:]
        else:
            kept.append(have.reshape(-1, 2 * hw))
    mine = jnp.concatenate(kept, axis=0)
    theirs = swap_seq(mine, 1)
    marks = jnp.concatenate([mine[1024:], theirs[1024:]], axis=0)
    marks = marks.reshape(64, 16, 2 * hw)[:, 8, 0:8].astype(jnp.int32)
    all_pos = (marks[:, 0:4] * 64 + marks[:, 4:8]).reshape(64 * slots, 1)
    bias = key_flags(idx, all_pos)

    tile_w = vit_qkv.reshape(vit_qkv.shape[0], 3 * width)
    gain = vit_gain.reshape(4, 1, width)
    rows = [
        encode(idx, chunk, a, b, c, d, gain, tile_w)
        for chunk, (a, b), (c, d) in zip(chunks, near, far)
    ]
    proj_here = lax.dynamic_slice_in_dim(tile_proj, mp * width, width, 0)
    joined = jnp.concatenate([dot(vit_out, tile_proj).astype(BF), proj_here], axis=0)
    partial = dot(jnp.concatenate(rows, axis=0).astype(BF), joined)
    shares = [partial] + [shift_mp(partial, k) for k in (1, 3, 2)]
    tail = jnp.zeros((slots, 64), F32).at[:, 0].set(high).at[:, 1].set(low).astype(BF)
    emb = embed_rows(shares, tail, gain_row, slide_w)
    emb = lax.all_to_all(jnp.broadcast_to(emb[None], (64,) + emb.shape), "seq", 0, 0)
    emb = emb.reshape(64 * slots, emb.shape[2])

    out_w = long_out.reshape(hw, 4, hw).transpose(1, 0, 2)
    o0, o1, o2, o3 = attend(idx, q_cache, mine, theirs, bias, emb, out_w)
    terms = [o0, shift_mp(o1, 1), shift_mp(o2, 2), shift_mp(o3, 3)]
    return pl.pallas_call(
        combine_kernel,
        out_shape=jax.ShapeDtypeStruct((ROWS, hw), BF),
        in_specs=[whole()] * 4,
        out_specs=whole(),
        name="combine",
    )(*terms)


def solution(mesh):
    placed = (
        P("seq", None, "mp"),
        P("seq"),
        P("seq"),
        P(),
        P(None, None, "mp"),
        P("mp", None),
        P(),
        P("seq", None),
        P(),
        P(None, None, "mp"),
        P("mp", None),
    )
    return jax.shard_map(
        local, mesh=mesh, in_specs=placed, out_specs=P("seq", "mp"), check_vma=False
    )
```

```python
import functools
import math

import jax
import jax.numpy as jnp
from jax import lax
from jax.experimental import pallas as pl
from jax.experimental.pallas import tpu as pltpu
from jax.sharding import PartitionSpec as P

HDT = 64
HDL = 48
BRANCHES = 5
EPSILON = 1e-05
FLOOR_SCORE = -1e30
BF = jnp.bfloat16
F32 = jnp.float32
ROWS = 128
NEAR = 3
NEAR_ROWS = 224


def params(mib=40):
    return pltpu.CompilerParams(vmem_limit_bytes=mib * 2**20)


def whole(kind=pltpu.VMEM):
    return pl.BlockSpec(memory_space=kind)


def dot(a, b):
    return jnp.dot(a, b, preferred_element_type=F32)


def dot_t(a, b):
    return lax.dot_general(a, b, (((1,), (1,)), ((), ())), preferred_element_type=F32)


def iota(shape, dim):
    return lax.broadcasted_iota(jnp.int32, shape, dim)


def encode_kernel(idx, own, left, right, far, gain, weight, out, xn, qk):
    mp = idx[0]
    tokens, width = own.shape[1], own.shape[2]
    unit = HDT ** (-0.5) * math.log2(math.e)
    features = 4 * width
    blocks = [lax.rem(mp + shift, 4) for shift in (0, 3, 1, 2)]
    starts = [pl.multiple_of(block * width, 128) for block in blocks]
    for t in range(2):
        parts = [own[t], left[t], right[t], far[t]]
        wide = [part.astype(F32) for part in parts]
        total = sum(jnp.sum(part, axis=-1, keepdims=True) for part in wide)
        mean = total * (1.0 / features)
        centred = [part - mean for part in wide]
        spread = sum(jnp.sum(part * part, axis=-1, keepdims=True) for part in centred)
        scale = lax.rsqrt(spread * (1.0 / features) + EPSILON)
        for d in range(4):
            xn[d, t * tokens : (t + 1) * tokens, :] = (
                centred[d] * scale * gain[pl.ds(blocks[d], 1), 0, :]
            ).astype(BF)
        out[t : t + 1, width : 2 * width] = jnp.sum(wide[0], axis=0, keepdims=True) * (1.0 / tokens)
    for part in range(2):
        acc = dot(xn[0], weight[part, pl.ds(starts[0], width), :])
        for d in range(1, 4):
            acc = acc + dot(xn[d], weight[part, pl.ds(starts[d], width), :])
        qk[:, part * width : (part + 1) * width] = acc.astype(BF)
    lane = iota((tokens, 2 * HDT), 1)
    pooled = [[] for _ in range(4)]
    for t in range(2):
        low, high = t * tokens, (t + 1) * tokens
        rows = []
        for pair in range(width // (2 * HDT)):
            q2 = qk[low:high, pair * 128 : (pair + 1) * 128]
            k2 = qk[low:high, width + pair * 128 : width + (pair + 1) * 128]
            for half in range(2):
                qm = jnp.where((lane >= HDT) == (half == 1), q2, jnp.zeros((), BF))
                s = dot_t(qm, k2)
                e = jnp.exp2((s - jnp.max(s, axis=-1, keepdims=True)) * unit)
                share = 1.0 / (jnp.sum(e, axis=-1, keepdims=True) * tokens)
                rows.append(jnp.sum(e * share, axis=0, keepdims=True))
        rows.append(jnp.zeros((8 - len(rows), tokens), F32))
        mix = jnp.concatenate(rows, axis=0).astype(BF)
        for d in range(4):
            pooled[d].append(dot(mix, xn[d, low:high, :]))
    acc = jnp.zeros((16, width), F32)
    for d in range(4):
        acc = acc + dot(
            jnp.concatenate(pooled[d], axis=0).astype(BF),
            weight[2, pl.ds(starts[d], width), :],
        )
    keep = (iota((16, width), 0) & 7) == (iota((16, width), 1) >> 6)
    acc = jnp.where(keep, acc, 0.0)
    for t in range(2):
        out[t : t + 1, 0:width] = jnp.sum(acc[t * 8 : (t + 1) * 8], axis=0, keepdims=True)


def encode(idx, chunk, own, left, right, far, gain, weight):
    tokens, width = own.shape[1], own.shape[2]
    block = pl.BlockSpec((2, tokens, width), lambda i: (chunk, 0, 0))
    far_block = pl.BlockSpec((2, tokens, width), lambda i: (0, 0, 0))
    return pl.pallas_call(
        encode_kernel,
        grid=(1,),
        out_shape=jax.ShapeDtypeStruct((2, 2 * width), F32),
        in_specs=[whole(pltpu.SMEM), block, block, block, far_block] + [whole()] * 2,
        out_specs=whole(),
        scratch_shapes=[
            pltpu.VMEM((4, 2 * tokens, width), BF),
            pltpu.VMEM((2 * tokens, 2 * width), BF),
        ],
        compiler_params=params(),
        cost_estimate=pl.CostEstimate(
            flops=6 * 10**9, bytes_accessed=8 * 10**6, transcendentals=8 * 10**5
        ),
        name="encode",
    )(idx, own, left, right, far, gain, weight)


def norm_rows(x, gain):
    mean = jnp.mean(x, axis=-1, keepdims=True)
    centre = x - mean
    spread = jnp.mean(centre * centre, axis=-1, keepdims=True)
    return (centre * lax.rsqrt(spread + EPSILON) * gain).astype(BF)


def slot_digits(idx, slot):
    place = jnp.where(slot < idx[2], idx[3 + slot], -64)
    return (place >> 6).astype(F32), (place & 63).astype(F32)


def embed_kernel(idx, a, b, c, d, gain, weight, out):
    width = weight.shape[0]
    third = width // 3
    total = (a[...] + b[...]) + (c[...] + d[...])
    normed = norm_rows(total.astype(BF).astype(F32), gain[...])
    out[:, 0 : 2 * third] = dot_t(normed, weight[third:, :]).astype(BF)
    out[:, 2 * third : width] = dot_t(normed, weight[0:third, :]).astype(BF)
    shape = (out.shape[0], out.shape[1] - width)
    row, column = iota(shape, 0), iota(shape, 1)
    tail = jnp.zeros(shape, F32)
    for slot in range(shape[0]):
        high, low = slot_digits(idx, slot)
        tail = jnp.where((row == slot) & (column == 0), high, tail)
        tail = jnp.where((row == slot) & (column == 1), low, tail)
    out[:, width:] = tail.astype(BF)


def embed_rows(idx, parts, gain, weight):
    rows, width = parts[0].shape[0], weight.shape[0]
    return pl.pallas_call(
        embed_kernel,
        out_shape=jax.ShapeDtypeStruct((rows, width + 64), BF),
        in_specs=[whole(pltpu.SMEM)] + [whole()] * 6,
        out_specs=whole(),
        compiler_params=params(),
        name="embed_rows",
    )(idx, *parts, gain, weight)


def rev4(x):
    return ((x & 1) << 3) | ((x & 2) << 1) | ((x & 4) >> 1) | ((x & 8) >> 3)


def pick_start(head, level):
    return pl.multiple_of((rev4(head & 15) >> (4 - level)) * (ROWS >> level), 8)


def local_row(j, level, head):
    bits = j >> 3
    free = 4 - level
    turned = rev4(bits) >> (4 - free) if free else bits * 0
    return (j & 7) * 16 + (turned << level) + (head & ((1 << level) - 1))


def slide_kernel(idx, cache, gain, weight, q_out, near, light, kv):
    heads_width = q_out.shape[1]
    first_head = idx[0] * 4
    row = iota((ROWS, ROWS), 0)
    turn = (local_row(row, 0, 0) == iota((ROWS, ROWS), 1)).astype(BF)
    normed = norm_rows(cache[...].astype(F32), gain[...])
    normed = dot(turn, normed).astype(BF)
    q_out[...] = dot_t(normed, weight[0:heads_width, :]).astype(BF).astype(F32)
    kv[...] = dot_t(normed, weight[heads_width:, :]).astype(BF).astype(F32)
    base = 0
    for level in range(BRANCHES):
        n = ROWS >> level
        column = iota((n, 2 * heads_width), 1)
        column = jnp.where(column >= heads_width, column - heads_width, column)
        got = jnp.zeros((n, 2 * heads_width), F32)
        for h in range(4):
            here = (column >= h * HDL) & (column < (h + 1) * HDL)
            got = jnp.where(here, kv[pl.ds(pick_start(first_head + h, level), n), :], got)
        if level == BRANCHES - 1:
            lane = iota((8, 2 * heads_width), 1)
            tail = jnp.zeros((8, 2 * heads_width), F32)
            for slot in range(4):
                high, low = slot_digits(idx, slot)
                tail = jnp.where(lane == slot, high, jnp.where(lane == slot + 4, low, tail))
            got = jnp.concatenate([got, tail], axis=0)
        picks = near if level < NEAR else light
        base = 0 if level == NEAR else base
        picks[base : base + got.shape[0], :] = got.astype(BF)
        base += n


def slide_project(idx, cache, gain, weight):
    hw = weight.shape[0] // 3
    return pl.pallas_call(
        slide_kernel,
        out_shape=(
            jax.ShapeDtypeStruct((ROWS, hw), F32),
            jax.ShapeDtypeStruct((NEAR_ROWS, 2 * hw), BF),
            jax.ShapeDtypeStruct((32, 2 * hw), BF),
        ),
        in_specs=[whole(pltpu.SMEM)] + [whole()] * 3,
        out_specs=(whole(),) * 3,
        scratch_shapes=[pltpu.VMEM((ROWS, 2 * hw), F32)],
        compiler_params=params(),
        name="slide_project",
    )(idx, cache, gain, weight)


def flag_kernel(idx, pos, out):
    first_head, seq = idx[0] * 4, idx[1]
    for level in range(BRANCHES):
        last = level == BRANCHES - 1
        keys = 1024 if last else 512
        n = 16 if last else ROWS >> level
        shift = n.bit_length() - 1
        k = iota((8, keys), 1)
        j = k & (n - 1)
        source = (seq & -(4 << level)) + (k >> shift)
        for h in range(4):
            r = level * 8 + h
            if level == 0 and h > 0:
                out[r : r + 1, 0:keys] = out[0:1, 0:keys]
                continue
            place = source * ROWS + local_row(j & 7 if last else j, level, first_head + h)
            hit = jnp.max(jnp.where(pos[...] == place[0:1], 1.0, 0.0), axis=0, keepdims=True)
            gone = (hit > 0.0) | (j[0:1] >= 8) if last else hit > 0.0
            out[r : r + 1, 0:keys] = jnp.where(gone, FLOOR_SCORE, 0.0)


def key_flags(idx, pos):
    return pl.pallas_call(
        flag_kernel,
        out_shape=jax.ShapeDtypeStruct((8 * BRANCHES, 1024), F32),
        in_specs=[whole(pltpu.SMEM), whole()],
        out_specs=whole(),
        compiler_params=params(),
        name="key_flags",
    )(idx, pos)


def depth_of(x):
    return sum(((x & mask) == 0).astype(jnp.int32) for mask in (1, 3, 7, 15))


def attend_kernel(
    idx, q_cache, group, light, bias, emb, out_w, o0, o1, o2, o3, q, kv, peak, total, acc, sems
):
    mp, seq = idx[0], idx[1]
    first_head = mp * 4
    hw = q_cache.shape[1]
    scale = HDL ** (-0.5)
    slots = emb.shape[0]
    copies = [[] for _ in range(NEAR)]
    sem = 0
    for level in range(NEAR):
        shards, n = 4 << level, ROWS >> level
        begin = (seq & 15) & -shards
        first_row = sum(ROWS >> b for b in range(level))
        for i in range(shards):
            at = pl.multiple_of((begin + i) * NEAR_ROWS + first_row, 16)
            copy = pltpu.make_async_copy(
                group.at[pl.ds(at, n)],
                kv.at[pl.ds(level * 512 + i * n, n)],
                sems.at[sem],
            )
            copy.start()
            copies[level].append(copy)
            sem += 1
    for i in range(32):
        kv[1536 + i * 16 : 1552 + i * 16, :] = light[(seq & 32) + i, 0:16, :]
    for i in range(64):
        kv[2048 + i * 16 : 2064 + i * 16, :] = light[i, 16:32, :]
    tail = emb[:, 3 * hw :]
    col = iota((8, tail.shape[1]), 1)
    digits = jnp.where(col == 0, 64.0, jnp.where(col == 1, 1.0, 0.0)).astype(BF)
    pos = dot_t(digits, tail).astype(jnp.int32)[0:1]
    own = seq * ROWS + local_row(iota((ROWS, 1), 0), 0, 0)
    match = own == pos
    found = jnp.max(match.astype(jnp.int32), axis=1, keepdims=True) > 0
    placed = dot(match.astype(BF), emb[:, 2 * hw : 3 * hw])
    q[...] = jnp.where(found, placed, q_cache[...])

    def head_mask(n, h):
        column = iota((n, hw), 1)
        return (column >= h * HDL) & (column < (h + 1) * HDL)

    def queries(level):
        n = ROWS >> level
        got = []
        for h in range(4):
            rows = q[...] if level == 0 else q[pl.ds(pick_start(first_head + h, level), n), :]
            got.append(jnp.where(head_mask(n, h), rows, 0.0))
        return jnp.concatenate(got, axis=0).astype(BF)

    full_q = queries(0)
    s = dot_t(full_q, emb[:, 0:hw]) * scale
    cross = (pos ^ (seq * ROWS)) >> 9
    first = sum(((cross >> b) != 0).astype(jnp.int32) for b in range(4))
    times = []
    for h in range(4):
        q_depth = depth_of(own ^ (first_head + h))
        k_depth = jnp.where(pos < 0, -1, depth_of(pos ^ (first_head + h)) - first)
        times.append(jnp.maximum(jnp.minimum(k_depth, q_depth - first) + 1, 0))
    times = jnp.concatenate(times, axis=0).astype(F32)
    s = jnp.where(times > 0.0, s, FLOOR_SCORE)
    m = jnp.max(s, axis=-1, keepdims=True)
    e = times * jnp.exp(s - m)
    peak[...] = jnp.broadcast_to(m, peak.shape)
    total[...] = jnp.broadcast_to(jnp.sum(e, axis=-1, keepdims=True), total.shape)
    acc[...] = dot(e.astype(BF), emb[:, hw : 2 * hw])

    for level in range(BRANCHES):
        n = ROWS >> level
        qb = full_q if level == 0 else queries(level)
        for copy in copies[level] if level < NEAR else ():
            copy.wait()
        low, keys = 512 * level, 1024 if level == BRANCHES - 1 else 512
        s = dot_t(qb, kv[low : low + keys, 0:hw]) * scale
        s = s.reshape(4, n, keys) + bias[level * 8 : level * 8 + 4, 0:keys][:, None, :]
        s = s.reshape(4 * n, keys)
        m = jnp.max(s, axis=-1, keepdims=True)
        e = jnp.exp(s - m)
        t = jnp.sum(e, axis=-1, keepdims=True)
        o = dot(e.astype(BF), kv[low : low + keys, hw : 2 * hw])
        for h in range(4):
            start = h * ROWS + (0 if level == 0 else pick_start(first_head + h, level))
            at = pl.ds(pl.multiple_of(start, 8), n)
            part = slice(h * n, (h + 1) * n)
            before = peak[at, :]
            after = jnp.maximum(before, m[part])
            keep, add = jnp.exp(before - after), jnp.exp(m[part] - after)
            peak[at, :] = after
            total[at, :] = total[at, :] * keep + t[part] * add
            acc[at, :] = acc[at, :] * keep[:, 0:1] + o[part] * add[:, 0:1]

    attended = jnp.zeros((ROWS, hw), F32)
    for h in range(4):
        rows = slice(h * ROWS, (h + 1) * ROWS)
        attended = jnp.where(head_mask(ROWS, h), acc[rows, :] / total[rows, 0:1], attended)
    turn = (local_row(iota((ROWS, ROWS), 1), 0, 0) == iota((ROWS, ROWS), 0)).astype(BF)
    attended = dot(turn, attended.astype(BF)).astype(BF)
    for d, o in enumerate((o0, o1, o2, o3)):
        o[...] = dot(attended, out_w[lax.rem(mp + d, 4)]).astype(BF)


def attend(idx, q_cache, group, light, bias, emb, out_w):
    hw = q_cache.shape[1]
    return pl.pallas_call(
        attend_kernel,
        out_shape=(jax.ShapeDtypeStruct((ROWS, hw), BF),) * 4,
        in_specs=[whole(pltpu.SMEM), whole(), whole(pl.ANY)] + [whole()] * 4,
        out_specs=(whole(),) * 4,
        scratch_shapes=[
            pltpu.VMEM((ROWS, hw), F32),
            pltpu.VMEM((3072, 2 * hw), BF),
            pltpu.VMEM((4 * ROWS, 128), F32),
            pltpu.VMEM((4 * ROWS, 128), F32),
            pltpu.VMEM((4 * ROWS, hw), F32),
            pltpu.SemaphoreType.DMA((28,)),
        ],
        compiler_params=params(),
        name="attend",
    )(idx, q_cache, group, light, bias, emb, out_w)


def shift_mp(x, k):
    return lax.ppermute(x, "mp", [(i, (i + k) % 4) for i in range(4)])


def local(
    tile_batch,
    positions,
    counts,
    vit_gain,
    vit_qkv,
    vit_out,
    tile_proj,
    seq_cache,
    long_gain,
    long_qkv,
    long_out,
):
    mp, seq = lax.axis_index("mp"), lax.axis_index("seq")
    idx = jnp.concatenate([jnp.stack([mp, seq]).astype(jnp.int32), counts, positions])
    slots, _, width = tile_batch.shape
    model = seq_cache.shape[1]
    hw = long_qkv.shape[-1]

    left, right = shift_mp(tile_batch, 1), shift_mp(tile_batch, 3)
    far = [shift_mp(left[0:2], 1), shift_mp(right[2:4], 3)]

    slide_w = long_qkv.transpose(1, 2, 0).reshape(3 * hw, model)
    gain_row = long_gain.reshape(1, model)
    q_cache, heavy, light = slide_project(idx, seq_cache, gain_row, slide_w)
    light = lax.all_to_all(jnp.broadcast_to(light[None], (64,) + light.shape), "seq", 0, 0)
    groups = [[16 * g + i for i in range(16)] for g in range(4)]
    group = lax.all_gather(heavy, "seq", axis=0, tiled=True, axis_index_groups=groups)
    marks = light[:, 24, 0:8].astype(jnp.int32)
    all_pos = (marks[:, 0:4] * 64 + marks[:, 4:8]).reshape(64 * slots, 1)
    bias = key_flags(idx, all_pos)

    tile_w = vit_qkv.transpose(1, 0, 2)
    gain = vit_gain.reshape(4, 1, width)
    rows = [encode(idx, i, tile_batch, left, right, far[i], gain, tile_w) for i in range(2)]
    proj_here = lax.dynamic_slice_in_dim(tile_proj, mp * width, width, 0)
    joined = jnp.concatenate([dot(vit_out, tile_proj).astype(BF), proj_here], axis=0)
    partial = dot(jnp.concatenate(rows, axis=0).astype(BF), joined)
    shares = [partial] + [shift_mp(partial, k) for k in (1, 3, 2)]
    emb = embed_rows(idx, shares, gain_row, slide_w)
    emb, bias = lax.optimization_barrier((emb, bias))
    emb = lax.all_to_all(jnp.broadcast_to(emb[None], (64,) + emb.shape), "seq", 0, 0)
    emb = emb.reshape(64 * slots, emb.shape[2])

    out_w = long_out.reshape(hw, 4, hw).transpose(1, 0, 2)
    o0, o1, o2, o3 = attend(idx, q_cache, group, light, bias, emb, out_w)
    terms = [o0, shift_mp(o1, 1), shift_mp(o2, 2), shift_mp(o3, 3)]
    a, b, c, d = [term.astype(F32) for term in terms]
    return ((a + b) + (c + d)).astype(BF)


def solution(mesh):
    placed = (
        P("seq", None, "mp"),
        P("seq"),
        P("seq"),
        P(),
        P(None, None, "mp"),
        P("mp", None),
        P(),
        P("seq", None),
        P(),
        P(None, None, "mp"),
        P("mp", None),
    )
    return jax.shard_map(
        local, mesh=mesh, in_specs=placed, out_specs=P("seq", "mp"), check_vma=False
    )
```

```python
import functools
import math

import jax
import jax.numpy as jnp
from jax import lax
from jax.experimental import pallas as pl
from jax.experimental.pallas import tpu as pltpu
from jax.sharding import PartitionSpec as P

HDT = 64
HDL = 48
BRANCHES = 5
EPSILON = 1e-05
FLOOR_SCORE = -1e30
BF = jnp.bfloat16
F32 = jnp.float32
ROWS = 128
BASES = (0, 256, 512, 768, 1024)


def params(mib=40):
    return pltpu.CompilerParams(vmem_limit_bytes=mib * 2**20)


def whole(kind=pltpu.VMEM):
    return pl.BlockSpec(memory_space=kind)


def dot(a, b):
    return jnp.dot(a, b, preferred_element_type=F32)


def dot_t(a, b):
    return lax.dot_general(a, b, (((1,), (1,)), ((), ())), preferred_element_type=F32)


def iota(shape, dim):
    return lax.broadcasted_iota(jnp.int32, shape, dim)


def encode_kernel(idx, own, left, right, far, gain, weight, out, xn, qk):
    mp = idx[0]
    tokens, width = own.shape[1], own.shape[2]
    unit = HDT ** (-0.5) * math.log2(math.e)
    features = 4 * width
    blocks = [lax.rem(mp + shift, 4) for shift in (0, 3, 1, 2)]
    starts = [pl.multiple_of(block * width, 128) for block in blocks]
    for t in range(2):
        parts = [own[t], left[t], right[t], far[t]]
        wide = [part.astype(F32) for part in parts]
        total = sum(jnp.sum(part, axis=-1, keepdims=True) for part in wide)
        mean = total * (1.0 / features)
        centred = [part - mean for part in wide]
        spread = sum(jnp.sum(part * part, axis=-1, keepdims=True) for part in centred)
        scale = lax.rsqrt(spread * (1.0 / features) + EPSILON)
        for d in range(4):
            xn[d, t * tokens : (t + 1) * tokens, :] = (
                centred[d] * scale * gain[pl.ds(blocks[d], 1), 0, :]
            ).astype(BF)
        out[t : t + 1, width : 2 * width] = jnp.sum(wide[0], axis=0, keepdims=True) * (1.0 / tokens)
    for part in range(2):
        acc = dot(xn[0], weight[part, pl.ds(starts[0], width), :])
        for d in range(1, 4):
            acc = acc + dot(xn[d], weight[part, pl.ds(starts[d], width), :])
        qk[:, part * width : (part + 1) * width] = acc.astype(BF)
    lane = iota((tokens, 2 * HDT), 1)
    pooled = [[] for _ in range(4)]
    for t in range(2):
        low, high = t * tokens, (t + 1) * tokens
        rows = []
        for pair in range(width // (2 * HDT)):
            q2 = qk[low:high, pair * 128 : (pair + 1) * 128]
            k2 = qk[low:high, width + pair * 128 : width + (pair + 1) * 128]
            for half in range(2):
                qm = jnp.where((lane >= HDT) == (half == 1), q2, jnp.zeros((), BF))
                s = dot_t(qm, k2)
                e = jnp.exp2((s - jnp.max(s, axis=-1, keepdims=True)) * unit)
                share = 1.0 / (jnp.sum(e, axis=-1, keepdims=True) * tokens)
                rows.append(jnp.sum(e * share, axis=0, keepdims=True))
        rows.append(jnp.zeros((8 - len(rows), tokens), F32))
        mix = jnp.concatenate(rows, axis=0).astype(BF)
        for d in range(4):
            pooled[d].append(dot(mix, xn[d, low:high, :]))
    acc = jnp.zeros((16, width), F32)
    for d in range(4):
        acc = acc + dot(
            jnp.concatenate(pooled[d], axis=0).astype(BF),
            weight[2, pl.ds(starts[d], width), :],
        )
    keep = (iota((16, width), 0) & 7) == (iota((16, width), 1) >> 6)
    acc = jnp.where(keep, acc, 0.0)
    for t in range(2):
        out[t : t + 1, 0:width] = jnp.sum(acc[t * 8 : (t + 1) * 8], axis=0, keepdims=True)


def encode(idx, chunk, own, left, right, far, gain, weight):
    tokens, width = own.shape[1], own.shape[2]
    block = pl.BlockSpec((2, tokens, width), lambda i: (chunk, 0, 0))
    far_block = pl.BlockSpec((2, tokens, width), lambda i: (0, 0, 0))
    return pl.pallas_call(
        encode_kernel,
        grid=(1,),
        out_shape=jax.ShapeDtypeStruct((2, 2 * width), F32),
        in_specs=[whole(pltpu.SMEM), block, block, block, far_block] + [whole()] * 2,
        out_specs=whole(),
        scratch_shapes=[
            pltpu.VMEM((4, 2 * tokens, width), BF),
            pltpu.VMEM((2 * tokens, 2 * width), BF),
        ],
        compiler_params=params(),
        cost_estimate=pl.CostEstimate(
            flops=6 * 10**9, bytes_accessed=8 * 10**6, transcendentals=8 * 10**5
        ),
        name="encode",
    )(idx, own, left, right, far, gain, weight)


def norm_rows(x, gain):
    mean = jnp.mean(x, axis=-1, keepdims=True)
    centre = x - mean
    spread = jnp.mean(centre * centre, axis=-1, keepdims=True)
    return (centre * lax.rsqrt(spread + EPSILON) * gain).astype(BF)


def slot_digits(idx, slot):
    place = jnp.where(slot < idx[2], idx[3 + slot], -64)
    return (place >> 6).astype(F32), (place & 63).astype(F32)


def embed_kernel(idx, a, b, c, d, gain, weight, out):
    width = weight.shape[0]
    third = width // 3
    total = (a[...] + b[...]) + (c[...] + d[...])
    normed = norm_rows(total.astype(BF).astype(F32), gain[...])
    out[:, 0 : 2 * third] = dot_t(normed, weight[third:, :]).astype(BF)
    out[:, 2 * third : width] = dot_t(normed, weight[0:third, :]).astype(BF)
    shape = (out.shape[0], out.shape[1] - width)
    row, column = iota(shape, 0), iota(shape, 1)
    tail = jnp.zeros(shape, F32)
    for slot in range(shape[0]):
        high, low = slot_digits(idx, slot)
        tail = jnp.where((row == slot) & (column == 0), high, tail)
        tail = jnp.where((row == slot) & (column == 1), low, tail)
    out[:, width:] = tail.astype(BF)


def embed_rows(idx, parts, gain, weight):
    rows, width = parts[0].shape[0], weight.shape[0]
    return pl.pallas_call(
        embed_kernel,
        out_shape=jax.ShapeDtypeStruct((rows, width + 64), BF),
        in_specs=[whole(pltpu.SMEM)] + [whole()] * 6,
        out_specs=whole(),
        compiler_params=params(),
        name="embed_rows",
    )(idx, *parts, gain, weight)


def rev4(x):
    return ((x & 1) << 3) | ((x & 2) << 1) | ((x & 4) >> 1) | ((x & 8) >> 3)


def pick_start(head, level):
    return pl.multiple_of((rev4(head & 15) >> (4 - level)) * (ROWS >> level), 8)


def local_row(j, level, head):
    bits = j >> 3
    free = 4 - level
    turned = rev4(bits) >> (4 - free) if free else bits * 0
    return (j & 7) * 16 + (turned << level) + (head & ((1 << level) - 1))


def slide_kernel(idx, cache, gain, weight, q_out, picks, kv):
    heads_width = q_out.shape[1]
    first_head = idx[0] * 4
    row = iota((ROWS, ROWS), 0)
    turn = (local_row(row, 0, 0) == iota((ROWS, ROWS), 1)).astype(BF)
    normed = norm_rows(cache[...].astype(F32), gain[...])
    normed = dot(turn, normed).astype(BF)
    q_out[...] = dot_t(normed, weight[0:heads_width, :]).astype(BF).astype(F32)
    kv[...] = dot_t(normed, weight[heads_width:, :]).astype(BF).astype(F32)
    base = 0
    for level in range(BRANCHES):
        n = ROWS >> level
        column = iota((n, 2 * heads_width), 1)
        column = jnp.where(column >= heads_width, column - heads_width, column)
        got = jnp.zeros((n, 2 * heads_width), F32)
        for h in range(4):
            here = (column >= h * HDL) & (column < (h + 1) * HDL)
            got = jnp.where(here, kv[pl.ds(pick_start(first_head + h, level), n), :], got)
        if level == BRANCHES - 1:
            lane = iota((8, 2 * heads_width), 1)
            tail = jnp.zeros((8, 2 * heads_width), F32)
            for slot in range(4):
                high, low = slot_digits(idx, slot)
                tail = jnp.where(lane == slot, high, jnp.where(lane == slot + 4, low, tail))
            got = jnp.concatenate([got, tail], axis=0)
        picks[base : base + got.shape[0], :] = got.astype(BF)
        base += n


def slide_project(idx, cache, gain, weight):
    hw = weight.shape[0] // 3
    return pl.pallas_call(
        slide_kernel,
        out_shape=(
            jax.ShapeDtypeStruct((ROWS, hw), F32),
            jax.ShapeDtypeStruct((2 * ROWS, 2 * hw), BF),
        ),
        in_specs=[whole(pltpu.SMEM)] + [whole()] * 3,
        out_specs=(whole(),) * 2,
        scratch_shapes=[pltpu.VMEM((ROWS, 2 * hw), F32)],
        compiler_params=params(),
        name="slide_project",
    )(idx, cache, gain, weight)


def flag_kernel(idx, pos, out):
    first_head, seq = idx[0] * 4, idx[1]
    for level in range(BRANCHES):
        last = level == BRANCHES - 1
        keys = 1024 if last else 512
        n = 16 if last else ROWS >> level
        shift = n.bit_length() - 1
        k = iota((8, keys), 1)
        j = k & (n - 1)
        half = keys // 2
        source = seq ^ (2 * ((k & (half - 1)) >> shift) + (k >= half).astype(jnp.int32))
        for h in range(4):
            r = level * 8 + h
            if level == 0 and h > 0:
                out[r : r + 1, 0:keys] = out[0:1, 0:keys]
                continue
            place = source * ROWS + local_row(j & 7 if last else j, level, first_head + h)
            hit = jnp.max(jnp.where(pos[...] == place[0:1], 1.0, 0.0), axis=0, keepdims=True)
            gone = (hit > 0.0) | (j[0:1] >= 8) if last else hit > 0.0
            out[r : r + 1, 0:keys] = jnp.where(gone, FLOOR_SCORE, 0.0)


def key_flags(idx, pos):
    return pl.pallas_call(
        flag_kernel,
        out_shape=jax.ShapeDtypeStruct((8 * BRANCHES, 1024), F32),
        in_specs=[whole(pltpu.SMEM), whole()],
        out_specs=whole(),
        compiler_params=params(),
        name="key_flags",
    )(idx, pos)


def depth_of(x):
    return sum(((x & mask) == 0).astype(jnp.int32) for mask in (1, 3, 7, 15))


def attend_kernel(
    idx, q_cache, mine, theirs, bias, emb, out_w, o0, o1, o2, o3, q, peak, total, acc
):
    mp, seq = idx[0], idx[1]
    first_head = mp * 4
    hw = q_cache.shape[1]
    scale = HDL ** (-0.5)
    slots = emb.shape[0]
    tail = emb[:, 3 * hw :]
    col = iota((8, tail.shape[1]), 1)
    digits = jnp.where(col == 0, 64.0, jnp.where(col == 1, 1.0, 0.0)).astype(BF)
    pos = dot_t(digits, tail).astype(jnp.int32)[0:1]
    own = seq * ROWS + local_row(iota((ROWS, 1), 0), 0, 0)
    match = own == pos
    found = jnp.max(match.astype(jnp.int32), axis=1, keepdims=True) > 0
    placed = dot(match.astype(BF), emb[:, 2 * hw : 3 * hw])
    q[...] = jnp.where(found, placed, q_cache[...])

    def head_mask(n, h):
        column = iota((n, hw), 1)
        return (column >= h * HDL) & (column < (h + 1) * HDL)

    def queries(level):
        n = ROWS >> level
        got = []
        for h in range(4):
            rows = q[...] if level == 0 else q[pl.ds(pick_start(first_head + h, level), n), :]
            got.append(jnp.where(head_mask(n, h), rows, 0.0))
        return jnp.concatenate(got, axis=0).astype(BF)

    full_q = queries(0)
    s = dot_t(full_q, emb[:, 0:hw]) * scale
    cross = (pos ^ (seq * ROWS)) >> 9
    first = sum(((cross >> b) != 0).astype(jnp.int32) for b in range(4))
    times = []
    for h in range(4):
        q_depth = depth_of(own ^ (first_head + h))
        k_depth = jnp.where(pos < 0, -1, depth_of(pos ^ (first_head + h)) - first)
        times.append(jnp.maximum(jnp.minimum(k_depth, q_depth - first) + 1, 0))
    times = jnp.concatenate(times, axis=0).astype(F32)
    s = jnp.where(times > 0.0, s, FLOOR_SCORE)
    m = jnp.max(s, axis=-1, keepdims=True)
    e = times * jnp.exp(s - m)
    peak[...] = jnp.broadcast_to(m, peak.shape)
    total[...] = jnp.broadcast_to(jnp.sum(e, axis=-1, keepdims=True), total.shape)
    acc[...] = dot(e.astype(BF), emb[:, hw : 2 * hw])

    for level in range(BRANCHES):
        n = ROWS >> level
        qb = full_q if level == 0 else queries(level)
        half = 512 if level == BRANCHES - 1 else 256
        low = BASES[level]
        sides = []
        for number, side in enumerate((mine, theirs)):
            s = dot_t(qb, side[low : low + half, 0:hw]) * scale
            flags = bias[level * 8 : level * 8 + 4, number * half : (number + 1) * half]
            s = s.reshape(4, n, half) + flags[:, None, :]
            sides.append(s.reshape(4 * n, half))
        m = jnp.maximum(
            jnp.max(sides[0], axis=-1, keepdims=True), jnp.max(sides[1], axis=-1, keepdims=True)
        )
        e0, e1 = jnp.exp(sides[0] - m), jnp.exp(sides[1] - m)
        t = jnp.sum(e0, axis=-1, keepdims=True) + jnp.sum(e1, axis=-1, keepdims=True)
        o = dot(e0.astype(BF), mine[low : low + half, hw : 2 * hw]) + dot(
            e1.astype(BF), theirs[low : low + half, hw : 2 * hw]
        )
        for h in range(4):
            start = h * ROWS + (0 if level == 0 else pick_start(first_head + h, level))
            at = pl.ds(pl.multiple_of(start, 8), n)
            part = slice(h * n, (h + 1) * n)
            before = peak[at, :]
            after = jnp.maximum(before, m[part])
            keep, add = jnp.exp(before - after), jnp.exp(m[part] - after)
            peak[at, :] = after
            total[at, :] = total[at, :] * keep + t[part] * add
            acc[at, :] = acc[at, :] * keep[:, 0:1] + o[part] * add[:, 0:1]

    attended = jnp.zeros((ROWS, hw), F32)
    for h in range(4):
        rows = slice(h * ROWS, (h + 1) * ROWS)
        attended = jnp.where(head_mask(ROWS, h), acc[rows, :] / total[rows, 0:1], attended)
    turn = (local_row(iota((ROWS, ROWS), 1), 0, 0) == iota((ROWS, ROWS), 0)).astype(BF)
    attended = dot(turn, attended.astype(BF)).astype(BF)
    for d, o in enumerate((o0, o1, o2, o3)):
        o[...] = dot(attended, out_w[lax.rem(mp + d, 4)]).astype(BF)


def attend(idx, q_cache, mine, theirs, bias, emb, out_w):
    hw = q_cache.shape[1]
    return pl.pallas_call(
        attend_kernel,
        out_shape=(jax.ShapeDtypeStruct((ROWS, hw), BF),) * 4,
        in_specs=[whole(pltpu.SMEM)] + [whole()] * 6,
        out_specs=(whole(),) * 4,
        scratch_shapes=[
            pltpu.VMEM((ROWS, hw), F32),
            pltpu.VMEM((4 * ROWS, 128), F32),
            pltpu.VMEM((4 * ROWS, 128), F32),
            pltpu.VMEM((4 * ROWS, hw), F32),
        ],
        compiler_params=params(),
        name="attend",
    )(idx, q_cache, mine, theirs, bias, emb, out_w)


def shift_mp(x, k):
    return lax.ppermute(x, "mp", [(i, (i + k) % 4) for i in range(4)])


def swap_seq(x, bit):
    return lax.ppermute(x, "seq", [(i, i ^ bit) for i in range(64)])


def local(
    tile_batch,
    positions,
    counts,
    vit_gain,
    vit_qkv,
    vit_out,
    tile_proj,
    seq_cache,
    long_gain,
    long_qkv,
    long_out,
):
    mp, seq = lax.axis_index("mp"), lax.axis_index("seq")
    idx = jnp.concatenate([jnp.stack([mp, seq]).astype(jnp.int32), counts, positions])
    slots, _, width = tile_batch.shape
    model = seq_cache.shape[1]
    hw = long_qkv.shape[-1]

    left, right = shift_mp(tile_batch, 1), shift_mp(tile_batch, 3)
    tile_w = vit_qkv.transpose(1, 0, 2)
    gain = vit_gain.reshape(4, 1, width)

    slide_w = long_qkv.transpose(1, 2, 0).reshape(3 * hw, model)
    gain_row = long_gain.reshape(1, model)
    q_cache, picks = slide_project(idx, seq_cache, gain_row, slide_w)
    have = picks[None]
    kept = []
    for level, bit in enumerate((2, 4, 8, 16, 32)):
        have = jnp.concatenate([have, swap_seq(have, bit)], axis=0)
        n = ROWS >> level
        if level < BRANCHES - 1:
            kept.append(have[:, 0:n].reshape(-1, 2 * hw))
            have = have[:, n:]
        if level == 1:
            have, left, right = lax.optimization_barrier((have, left, right))
            far = [shift_mp(left[0:2], 1), shift_mp(right[2:4], 3)]
        if level == 2:
            have, *far = lax.optimization_barrier((have, *far))
        if level == 3:
            first = encode(idx, 0, tile_batch, left, right, far[0], gain, tile_w)
            have, first = lax.optimization_barrier((have, first))
    mine = jnp.concatenate(kept + [have.reshape(-1, 2 * hw)], axis=0)
    theirs = swap_seq(mine, 1)
    marks = jnp.concatenate([side[1024:].reshape(32, 16, 2 * hw)[:, 8, 0:8] for side in (mine, theirs)])
    marks = marks.astype(jnp.int32)
    all_pos = (marks[:, 0:4] * 64 + marks[:, 4:8]).reshape(64 * slots, 1)
    bias = key_flags(idx, all_pos)

    rows = [first, encode(idx, 1, tile_batch, left, right, far[1], gain, tile_w)]
    proj_here = lax.dynamic_slice_in_dim(tile_proj, mp * width, width, 0)
    joined = jnp.concatenate([dot(vit_out, tile_proj).astype(BF), proj_here], axis=0)
    partial = dot(jnp.concatenate(rows, axis=0).astype(BF), joined)
    shares = [partial] + [shift_mp(partial, k) for k in (1, 3, 2)]
    emb = embed_rows(idx, shares, gain_row, slide_w)
    emb, bias = lax.optimization_barrier((emb, bias))
    emb = lax.all_to_all(jnp.broadcast_to(emb[None], (64,) + emb.shape), "seq", 0, 0)
    emb = emb.reshape(64 * slots, emb.shape[2])

    out_w = long_out.reshape(hw, 4, hw).transpose(1, 0, 2)
    o0, o1, o2, o3 = attend(idx, q_cache, mine, theirs, bias, emb, out_w)
    terms = [o0, shift_mp(o1, 1), shift_mp(o2, 2), shift_mp(o3, 3)]
    a, b, c, d = [term.astype(F32) for term in terms]
    return ((a + b) + (c + d)).astype(BF)


def solution(mesh):
    placed = (
        P("seq", None, "mp"),
        P("seq"),
        P("seq"),
        P(),
        P(None, None, "mp"),
        P("mp", None),
        P(),
        P("seq", None),
        P(),
        P(None, None, "mp"),
        P("mp", None),
    )
    return jax.shard_map(
        local, mesh=mesh, in_specs=placed, out_specs=P("seq", "mp"), check_vma=False
    )
```

```python
import functools
import math

import jax
import jax.numpy as jnp
from jax import lax
from jax.experimental import pallas as pl
from jax.experimental.pallas import tpu as pltpu
from jax.sharding import PartitionSpec as P

HDT = 64
HDL = 48
BRANCHES = 5
EPSILON = 1e-05
FLOOR_SCORE = -1e30
BF = jnp.bfloat16
F32 = jnp.float32
ROWS = 128
BASES = (0, 256, 512, 768, 1024)


def params(mib=40):
    return pltpu.CompilerParams(vmem_limit_bytes=mib * 2**20)


def whole(kind=pltpu.VMEM):
    return pl.BlockSpec(memory_space=kind)


def dot(a, b):
    return jnp.dot(a, b, preferred_element_type=F32)


def dot_t(a, b):
    return lax.dot_general(a, b, (((1,), (1,)), ((), ())), preferred_element_type=F32)


def iota(shape, dim):
    return lax.broadcasted_iota(jnp.int32, shape, dim)


def encode_kernel(idx, own, left, right, far, gain, weight, out, xn, qk):
    mp = idx[0]
    tokens, width = own.shape[1], own.shape[2]
    unit = HDT ** (-0.5) * math.log2(math.e)
    features = 4 * width
    blocks = [lax.rem(mp + shift, 4) for shift in (0, 3, 1, 2)]
    starts = [pl.multiple_of(block * width, 128) for block in blocks]
    for t in range(2):
        parts = [own[t], left[t], right[t], far[t]]
        wide = [part.astype(F32) for part in parts]
        total = sum(jnp.sum(part, axis=-1, keepdims=True) for part in wide)
        mean = total * (1.0 / features)
        centred = [part - mean for part in wide]
        spread = sum(jnp.sum(part * part, axis=-1, keepdims=True) for part in centred)
        scale = lax.rsqrt(spread * (1.0 / features) + EPSILON)
        for d in range(4):
            xn[d, t * tokens : (t + 1) * tokens, :] = (
                centred[d] * scale * gain[pl.ds(blocks[d], 1), 0, :]
            ).astype(BF)
        out[t : t + 1, width : 2 * width] = jnp.sum(wide[0], axis=0, keepdims=True) * (1.0 / tokens)
    for part in range(2):
        acc = dot(xn[0], weight[part, pl.ds(starts[0], width), :])
        for d in range(1, 4):
            acc = acc + dot(xn[d], weight[part, pl.ds(starts[d], width), :])
        qk[:, part * width : (part + 1) * width] = acc.astype(BF)
    lane = iota((tokens, 2 * HDT), 1)
    pooled = [[] for _ in range(4)]
    for t in range(2):
        low, high = t * tokens, (t + 1) * tokens
        rows = []
        for pair in range(width // (2 * HDT)):
            q2 = qk[low:high, pair * 128 : (pair + 1) * 128]
            k2 = qk[low:high, width + pair * 128 : width + (pair + 1) * 128]
            for half in range(2):
                qm = jnp.where((lane >= HDT) == (half == 1), q2, jnp.zeros((), BF))
                s = dot_t(qm, k2)
                e = jnp.exp2((s - jnp.max(s, axis=-1, keepdims=True)) * unit)
                share = 1.0 / (jnp.sum(e, axis=-1, keepdims=True) * tokens)
                rows.append(jnp.sum(e * share, axis=0, keepdims=True))
        rows.append(jnp.zeros((8 - len(rows), tokens), F32))
        mix = jnp.concatenate(rows, axis=0).astype(BF)
        for d in range(4):
            pooled[d].append(dot(mix, xn[d, low:high, :]))
    acc = jnp.zeros((16, width), F32)
    for d in range(4):
        acc = acc + dot(
            jnp.concatenate(pooled[d], axis=0).astype(BF),
            weight[2, pl.ds(starts[d], width), :],
        )
    keep = (iota((16, width), 0) & 7) == (iota((16, width), 1) >> 6)
    acc = jnp.where(keep, acc, 0.0)
    for t in range(2):
        out[t : t + 1, 0:width] = jnp.sum(acc[t * 8 : (t + 1) * 8], axis=0, keepdims=True)


def encode(idx, chunk, own, left, right, far, gain, weight):
    tokens, width = own.shape[1], own.shape[2]
    block = pl.BlockSpec((2, tokens, width), lambda i: (chunk, 0, 0))
    far_block = pl.BlockSpec((2, tokens, width), lambda i: (0, 0, 0))
    return pl.pallas_call(
        encode_kernel,
        grid=(1,),
        out_shape=jax.ShapeDtypeStruct((2, 2 * width), F32),
        in_specs=[whole(pltpu.SMEM), block, block, block, far_block] + [whole()] * 2,
        out_specs=whole(),
        scratch_shapes=[
            pltpu.VMEM((4, 2 * tokens, width), BF),
            pltpu.VMEM((2 * tokens, 2 * width), BF),
        ],
        compiler_params=params(),
        cost_estimate=pl.CostEstimate(
            flops=6 * 10**9, bytes_accessed=8 * 10**6, transcendentals=8 * 10**5
        ),
        name="encode",
    )(idx, own, left, right, far, gain, weight)


def norm_rows(x, gain):
    mean = jnp.mean(x, axis=-1, keepdims=True)
    centre = x - mean
    spread = jnp.mean(centre * centre, axis=-1, keepdims=True)
    return (centre * lax.rsqrt(spread + EPSILON) * gain).astype(BF)


def slot_digits(idx, slot):
    place = jnp.where(slot < idx[2], idx[3 + slot], -64)
    return (place >> 6).astype(F32), (place & 63).astype(F32)


def embed_kernel(idx, a, b, c, d, gain, weight, out):
    width = weight.shape[0]
    third = width // 3
    total = (a[...] + b[...]) + (c[...] + d[...])
    normed = norm_rows(total.astype(BF).astype(F32), gain[...])
    out[:, 0 : 2 * third] = dot_t(normed, weight[third:, :]).astype(BF)
    out[:, 2 * third : width] = dot_t(normed, weight[0:third, :]).astype(BF)
    shape = (out.shape[0], out.shape[1] - width)
    row, column = iota(shape, 0), iota(shape, 1)
    tail = jnp.zeros(shape, F32)
    for slot in range(shape[0]):
        high, low = slot_digits(idx, slot)
        tail = jnp.where((row == slot) & (column == 0), high, tail)
        tail = jnp.where((row == slot) & (column == 1), low, tail)
    out[:, width:] = tail.astype(BF)


def embed_rows(idx, parts, gain, weight):
    rows, width = parts[0].shape[0], weight.shape[0]
    return pl.pallas_call(
        embed_kernel,
        out_shape=jax.ShapeDtypeStruct((rows, width + 64), BF),
        in_specs=[whole(pltpu.SMEM)] + [whole()] * 6,
        out_specs=whole(),
        compiler_params=params(),
        name="embed_rows",
    )(idx, *parts, gain, weight)


def rev4(x):
    return ((x & 1) << 3) | ((x & 2) << 1) | ((x & 4) >> 1) | ((x & 8) >> 3)


def pick_start(head, level):
    return pl.multiple_of((rev4(head & 15) >> (4 - level)) * (ROWS >> level), 8)


def local_row(j, level, head):
    bits = j >> 3
    free = 4 - level
    turned = rev4(bits) >> (4 - free) if free else bits * 0
    return (j & 7) * 16 + (turned << level) + (head & ((1 << level) - 1))


def slide_kernel(idx, cache, gain, weight, q_out, picks, kv):
    heads_width = q_out.shape[1]
    first_head = idx[0] * 4
    row = iota((ROWS, ROWS), 0)
    turn = (local_row(row, 0, 0) == iota((ROWS, ROWS), 1)).astype(BF)
    normed = norm_rows(cache[...].astype(F32), gain[...])
    normed = dot(turn, normed).astype(BF)
    q_out[...] = dot_t(normed, weight[0:heads_width, :]).astype(BF).astype(F32)
    kv[...] = dot_t(normed, weight[heads_width:, :]).astype(BF).astype(F32)
    base = 0
    for level in range(BRANCHES):
        n = ROWS >> level
        column = iota((n, 2 * heads_width), 1)
        column = jnp.where(column >= heads_width, column - heads_width, column)
        got = jnp.zeros((n, 2 * heads_width), F32)
        for h in range(4):
            here = (column >= h * HDL) & (column < (h + 1) * HDL)
            got = jnp.where(here, kv[pl.ds(pick_start(first_head + h, level), n), :], got)
        if level == BRANCHES - 1:
            got = jnp.concatenate([got, jnp.zeros((8, 2 * heads_width), F32)], axis=0)
        picks[base : base + got.shape[0], :] = got.astype(BF)
        base += n


def slide_project(idx, cache, gain, weight):
    hw = weight.shape[0] // 3
    return pl.pallas_call(
        slide_kernel,
        out_shape=(
            jax.ShapeDtypeStruct((ROWS, hw), F32),
            jax.ShapeDtypeStruct((2 * ROWS, 2 * hw), BF),
        ),
        in_specs=[whole(pltpu.SMEM)] + [whole()] * 3,
        out_specs=(whole(),) * 2,
        scratch_shapes=[pltpu.VMEM((ROWS, 2 * hw), F32)],
        compiler_params=params(),
        name="slide_project",
    )(idx, cache, gain, weight)


def depth_of(x):
    return sum(((x & mask) == 0).astype(jnp.int32) for mask in (1, 3, 7, 15))


def attend_kernel(
    idx, q_cache, mine_hbm, theirs_hbm, emb, out_w, o0, o1, o2, o3, q, mine, theirs, peak, total, acc, sems
):
    mp, seq = idx[0], idx[1]
    first_head = mp * 4
    hw = q_cache.shape[1]
    scale = HDL ** (-0.5)
    slots = emb.shape[0]
    loads = [
        pltpu.make_async_copy(mine_hbm, mine, sems.at[0]),
        pltpu.make_async_copy(theirs_hbm, theirs, sems.at[1]),
    ]
    for load in loads:
        load.start()
    tail = emb[:, 3 * hw :]
    col = iota((8, tail.shape[1]), 1)
    digits = jnp.where(col == 0, 64.0, jnp.where(col == 1, 1.0, 0.0)).astype(BF)
    pos = dot_t(digits, tail).astype(jnp.int32)[0:1]
    spread = dot_t(tail, digits).astype(jnp.int32)[:, 0:1]
    own = seq * ROWS + local_row(iota((ROWS, 1), 0), 0, 0)
    match = own == pos
    found = jnp.max(match.astype(jnp.int32), axis=1, keepdims=True) > 0
    placed = dot(match.astype(BF), emb[:, 2 * hw : 3 * hw])
    q[...] = jnp.where(found, placed, q_cache[...])

    def head_mask(n, h):
        column = iota((n, hw), 1)
        return (column >= h * HDL) & (column < (h + 1) * HDL)

    def queries(level):
        n = ROWS >> level
        got = []
        for h in range(4):
            rows = q[...] if level == 0 else q[pl.ds(pick_start(first_head + h, level), n), :]
            got.append(jnp.where(head_mask(n, h), rows, 0.0))
        return jnp.concatenate(got, axis=0).astype(BF)

    full_q = queries(0)
    s = dot_t(full_q, emb[:, 0:hw]) * scale
    cross = (pos ^ (seq * ROWS)) >> 9
    first = sum(((cross >> b) != 0).astype(jnp.int32) for b in range(4))
    times = []
    for h in range(4):
        q_depth = depth_of(own ^ (first_head + h))
        k_depth = jnp.where(pos < 0, -1, depth_of(pos ^ (first_head + h)) - first)
        times.append(jnp.maximum(jnp.minimum(k_depth, q_depth - first) + 1, 0))
    times = jnp.concatenate(times, axis=0).astype(F32)
    s = jnp.where(times > 0.0, s, FLOOR_SCORE)
    m = jnp.max(s, axis=-1, keepdims=True)
    e = times * jnp.exp(s - m)
    peak[...] = jnp.broadcast_to(m, peak.shape)
    total[...] = jnp.broadcast_to(jnp.sum(e, axis=-1, keepdims=True), total.shape)
    acc[...] = dot(e.astype(BF), emb[:, hw : 2 * hw])

    for load in loads:
        load.wait()
    for level in range(BRANCHES):
        n = ROWS >> level
        qb = full_q if level == 0 else queries(level)
        half = 512 if level == BRANCHES - 1 else 256
        low = BASES[level]
        last = level == BRANCHES - 1
        pitch = 16 if last else n
        turned = (rev4(spread & 15) << 3) + ((spread & 127) >> 4)
        cross_rows = (spread >> 7) ^ seq
        key = (cross_rows & 1) * half + (cross_rows >> 1) * pitch + (turned & (n - 1))
        inside = jnp.where((pos >= 0) & (first <= level), 1, 0)
        head_row = first_head + iota((8, slots), 0)
        hits = (((pos ^ head_row) & ((1 << level) - 1)) == 0) & (inside > 0)
        key_lane = iota((slots, 2 * half), 1)
        bias = dot(
            jnp.where(hits, FLOOR_SCORE, 0.0).astype(BF), (key_lane == key).astype(BF)
        )
        if last:
            bias = jnp.where((iota((8, 2 * half), 1) & 15) >= 8, FLOOR_SCORE, bias)
        sides = []
        for number, side in enumerate((mine, theirs)):
            s = dot_t(qb, side[low : low + half, 0:hw]) * scale
            flags = bias[0:4, number * half : (number + 1) * half]
            s = s.reshape(4, n, half) + flags[:, None, :]
            sides.append(s.reshape(4 * n, half))
        m = jnp.maximum(
            jnp.max(sides[0], axis=-1, keepdims=True), jnp.max(sides[1], axis=-1, keepdims=True)
        )
        e0, e1 = jnp.exp(sides[0] - m), jnp.exp(sides[1] - m)
        t = jnp.sum(e0, axis=-1, keepdims=True) + jnp.sum(e1, axis=-1, keepdims=True)
        o = dot(e0.astype(BF), mine[low : low + half, hw : 2 * hw]) + dot(
            e1.astype(BF), theirs[low : low + half, hw : 2 * hw]
        )
        for h in range(4):
            start = h * ROWS + (0 if level == 0 else pick_start(first_head + h, level))
            at = pl.ds(pl.multiple_of(start, 8), n)
            part = slice(h * n, (h + 1) * n)
            before = peak[at, :]
            after = jnp.maximum(before, m[part])
            keep, add = jnp.exp(before - after), jnp.exp(m[part] - after)
            peak[at, :] = after
            total[at, :] = total[at, :] * keep + t[part] * add
            acc[at, :] = acc[at, :] * keep[:, 0:1] + o[part] * add[:, 0:1]

    attended = jnp.zeros((ROWS, hw), F32)
    for h in range(4):
        rows = slice(h * ROWS, (h + 1) * ROWS)
        attended = jnp.where(head_mask(ROWS, h), acc[rows, :] / total[rows, 0:1], attended)
    turn = (local_row(iota((ROWS, ROWS), 1), 0, 0) == iota((ROWS, ROWS), 0)).astype(BF)
    attended = dot(turn, attended.astype(BF)).astype(BF)
    for d, o in enumerate((o0, o1, o2, o3)):
        o[...] = dot(attended, out_w[lax.rem(mp + d, 4)]).astype(BF)


def attend(idx, q_cache, mine, theirs, emb, out_w):
    hw = q_cache.shape[1]
    return pl.pallas_call(
        attend_kernel,
        out_shape=(jax.ShapeDtypeStruct((ROWS, hw), BF),) * 4,
        in_specs=[whole(pltpu.SMEM), whole()] + [whole(pl.ANY)] * 2 + [whole()] * 2,
        out_specs=(whole(),) * 4,
        scratch_shapes=[
            pltpu.VMEM((ROWS, hw), F32),
            pltpu.VMEM(mine.shape, BF),
            pltpu.VMEM(mine.shape, BF),
            pltpu.VMEM((4 * ROWS, 128), F32),
            pltpu.VMEM((4 * ROWS, 128), F32),
            pltpu.VMEM((4 * ROWS, hw), F32),
            pltpu.SemaphoreType.DMA((2,)),
        ],
        compiler_params=params(),
        name="attend",
    )(idx, q_cache, mine, theirs, emb, out_w)


def shift_mp(x, k):
    return lax.ppermute(x, "mp", [(i, (i + k) % 4) for i in range(4)])


def swap_seq(x, bit):
    return lax.ppermute(x, "seq", [(i, i ^ bit) for i in range(64)])


def local(
    tile_batch,
    positions,
    counts,
    vit_gain,
    vit_qkv,
    vit_out,
    tile_proj,
    seq_cache,
    long_gain,
    long_qkv,
    long_out,
):
    mp, seq = lax.axis_index("mp"), lax.axis_index("seq")
    idx = jnp.concatenate([jnp.stack([mp, seq]).astype(jnp.int32), counts, positions])
    slots, _, width = tile_batch.shape
    model = seq_cache.shape[1]
    hw = long_qkv.shape[-1]

    left, right = shift_mp(tile_batch, 1), shift_mp(tile_batch, 3)
    tile_w = vit_qkv.transpose(1, 0, 2)
    gain = vit_gain.reshape(4, 1, width)

    slide_w = long_qkv.transpose(1, 2, 0).reshape(3 * hw, model)
    gain_row = long_gain.reshape(1, model)
    q_cache, picks = slide_project(idx, seq_cache, gain_row, slide_w)
    proj_here = lax.dynamic_slice_in_dim(tile_proj, mp * width, width, 0)
    joined = jnp.concatenate([dot(vit_out, tile_proj).astype(BF), proj_here], axis=0)
    far = [shift_mp(left[0:2], 1), shift_mp(right[2:4], 3)]

    kept = []

    def step(have, level):
        have = jnp.concatenate([have, swap_seq(have, 2 << level)], axis=0)
        if level == BRANCHES - 1:
            return have
        n = ROWS >> level
        kept.append(have[:, 0:n].reshape(-1, 2 * hw))
        return have[:, n:]

    have = step(step(picks[None], 0), 1)
    far[0], have, joined = lax.optimization_barrier((far[0], have, joined))
    first = encode(idx, 0, tile_batch, left, right, far[0], gain, tile_w)
    have = step(have, 2)
    far[1], have, first = lax.optimization_barrier((far[1], have, first))
    second = encode(idx, 1, tile_batch, left, right, far[1], gain, tile_w)
    have = step(have, 3)
    first, second, have = lax.optimization_barrier((first, second, have))
    partial = dot(jnp.concatenate([first, second], axis=0).astype(BF), joined)
    shares = [partial] + [shift_mp(partial, k) for k in (1, 3, 2)]
    have = step(have, 4)
    mine = jnp.concatenate(kept + [have.reshape(-1, 2 * hw)], axis=0)
    shares, mine = lax.optimization_barrier((shares, mine))
    theirs = swap_seq(mine, 1)
    emb = embed_rows(idx, shares, gain_row, slide_w)
    emb = lax.all_to_all(jnp.broadcast_to(emb[None], (64,) + emb.shape), "seq", 0, 0)
    emb = emb.reshape(64 * slots, emb.shape[2])

    out_w = long_out.reshape(hw, 4, hw).transpose(1, 0, 2)
    o0, o1, o2, o3 = attend(idx, q_cache, mine, theirs, emb, out_w)
    terms = [o0, shift_mp(o1, 1), shift_mp(o2, 2), shift_mp(o3, 3)]
    a, b, c, d = [term.astype(F32) for term in terms]
    return ((a + b) + (c + d)).astype(BF)


def solution(mesh):
    placed = (
        P("seq", None, "mp"),
        P("seq"),
        P("seq"),
        P(),
        P(None, None, "mp"),
        P("mp", None),
        P(),
        P("seq", None),
        P(),
        P(None, None, "mp"),
        P("mp", None),
    )
    return jax.shard_map(
        local, mesh=mesh, in_specs=placed, out_specs=P("seq", "mp"), check_vma=False
    )
```

```python
import functools
import math

import jax
import jax.numpy as jnp
from jax import lax
from jax.experimental import pallas as pl
from jax.experimental.pallas import tpu as pltpu
from jax.sharding import PartitionSpec as P

HDT = 64
HDL = 48
BRANCHES = 5
EPSILON = 1e-05
FLOOR_SCORE = -1e30
BF = jnp.bfloat16
F32 = jnp.float32
ROWS = 128
BASES = (0, 256, 512, 768, 1024)


def params(mib=40):
    return pltpu.CompilerParams(vmem_limit_bytes=mib * 2**20)


def whole(kind=pltpu.VMEM):
    return pl.BlockSpec(memory_space=kind)


def dot(a, b):
    return jnp.dot(a, b, preferred_element_type=F32)


def dot_t(a, b):
    return lax.dot_general(a, b, (((1,), (1,)), ((), ())), preferred_element_type=F32)


def iota(shape, dim):
    return lax.broadcasted_iota(jnp.int32, shape, dim)


def encode_kernel(idx, own, left, right, far, gain, weight_hbm, out, weight, xn, qk, sems):
    mp = idx[0]
    tokens, width = own.shape[1], own.shape[2]
    unit = HDT ** (-0.5) * math.log2(math.e)
    features = 4 * width
    starts = [pl.multiple_of(lax.rem(mp + shift, 4) * width, 128) for shift in (0, 3, 1, 2)]
    loads = [
        pltpu.make_async_copy(weight_hbm.at[part], weight.at[part], sems.at[part])
        for part in range(3)
    ]
    for load in loads:
        load.start()
    for t in range(2):
        parts = [own[t], left[t], right[t], far[t]]
        wide = [part.astype(F32) for part in parts]
        total = sum(jnp.sum(part, axis=-1, keepdims=True) for part in wide)
        mean = total * (1.0 / features)
        centred = [part - mean for part in wide]
        spread = sum(jnp.sum(part * part, axis=-1, keepdims=True) for part in centred)
        scale = lax.rsqrt(spread * (1.0 / features) + EPSILON)
        for d in range(4):
            columns = pl.ds(starts[d], width)
            xn[t * tokens : (t + 1) * tokens, columns] = (
                centred[d] * scale * gain[:, columns]
            ).astype(BF)
        out[t : t + 1, width : 2 * width] = jnp.sum(wide[0], axis=0, keepdims=True) * (1.0 / tokens)
    for part in range(2):
        loads[part].wait()
        qk[:, part * width : (part + 1) * width] = dot(xn[...], weight[part]).astype(BF)
    lane = iota((tokens, 2 * HDT), 1)
    pooled = []
    for t in range(2):
        low, high = t * tokens, (t + 1) * tokens
        rows = []
        for pair in range(width // (2 * HDT)):
            q2 = qk[low:high, pair * 128 : (pair + 1) * 128]
            k2 = qk[low:high, width + pair * 128 : width + (pair + 1) * 128]
            for half in range(2):
                qm = jnp.where((lane >= HDT) == (half == 1), q2, jnp.zeros((), BF))
                s = dot_t(qm, k2)
                e = jnp.exp2((s - jnp.max(s, axis=-1, keepdims=True)) * unit)
                share = 1.0 / (jnp.sum(e, axis=-1, keepdims=True) * tokens)
                rows.append(jnp.sum(e * share, axis=0, keepdims=True))
        rows.append(jnp.zeros((8 - len(rows), tokens), F32))
        mix = jnp.concatenate(rows, axis=0).astype(BF)
        pooled.append(dot(mix, xn[low:high, :]))
    loads[2].wait()
    acc = dot(jnp.concatenate(pooled, axis=0).astype(BF), weight[2])
    keep = (iota((16, width), 0) & 7) == (iota((16, width), 1) >> 6)
    acc = jnp.where(keep, acc, 0.0)
    for t in range(2):
        out[t : t + 1, 0:width] = jnp.sum(acc[t * 8 : (t + 1) * 8], axis=0, keepdims=True)


def encode(idx, chunk, own, left, right, far, gain, weight):
    tokens, width = own.shape[1], own.shape[2]
    block = pl.BlockSpec((2, tokens, width), lambda i: (chunk, 0, 0))
    far_block = pl.BlockSpec((2, tokens, width), lambda i: (0, 0, 0))
    return pl.pallas_call(
        encode_kernel,
        grid=(1,),
        out_shape=jax.ShapeDtypeStruct((2, 2 * width), F32),
        in_specs=[whole(pltpu.SMEM), block, block, block, far_block, whole(), whole(pl.ANY)],
        out_specs=whole(),
        scratch_shapes=[
            pltpu.VMEM(weight.shape, BF),
            pltpu.VMEM((2 * tokens, 4 * width), BF),
            pltpu.VMEM((2 * tokens, 2 * width), BF),
            pltpu.SemaphoreType.DMA((3,)),
        ],
        compiler_params=params(),
        cost_estimate=pl.CostEstimate(
            flops=6 * 10**9, bytes_accessed=8 * 10**6, transcendentals=8 * 10**5
        ),
        name="encode",
    )(idx, own, left, right, far, gain, weight)


def norm_rows(x, gain):
    mean = jnp.mean(x, axis=-1, keepdims=True)
    centre = x - mean
    spread = jnp.mean(centre * centre, axis=-1, keepdims=True)
    return (centre * lax.rsqrt(spread + EPSILON) * gain).astype(BF)


def slot_digits(idx, slot):
    place = jnp.where(slot < idx[2], idx[3 + slot], -64)
    return (place >> 6).astype(F32), (place & 63).astype(F32)


def embed_kernel(idx, a, b, c, d, gain, weight, out):
    width = weight.shape[0]
    third = width // 3
    total = (a[...] + b[...]) + (c[...] + d[...])
    normed = norm_rows(total.astype(BF).astype(F32), gain[...])
    out[:, 0 : 2 * third] = dot_t(normed, weight[third:, :]).astype(BF)
    out[:, 2 * third : width] = dot_t(normed, weight[0:third, :]).astype(BF)
    shape = (out.shape[0], out.shape[1] - width)
    row, column = iota(shape, 0), iota(shape, 1)
    tail = jnp.zeros(shape, F32)
    for slot in range(shape[0]):
        high, low = slot_digits(idx, slot)
        tail = jnp.where((row == slot) & (column == 0), high, tail)
        tail = jnp.where((row == slot) & (column == 1), low, tail)
    out[:, width:] = tail.astype(BF)


def embed_rows(idx, parts, gain, weight):
    rows, width = parts[0].shape[0], weight.shape[0]
    return pl.pallas_call(
        embed_kernel,
        out_shape=jax.ShapeDtypeStruct((rows, width + 64), BF),
        in_specs=[whole(pltpu.SMEM)] + [whole()] * 6,
        out_specs=whole(),
        compiler_params=params(),
        name="embed_rows",
    )(idx, *parts, gain, weight)


def rev4(x):
    return ((x & 1) << 3) | ((x & 2) << 1) | ((x & 4) >> 1) | ((x & 8) >> 3)


def pick_start(head, level):
    return pl.multiple_of((rev4(head & 15) >> (4 - level)) * (ROWS >> level), 8)


def local_row(j, level, head):
    bits = j >> 3
    free = 4 - level
    turned = rev4(bits) >> (4 - free) if free else bits * 0
    return (j & 7) * 16 + (turned << level) + (head & ((1 << level) - 1))


def slide_kernel(idx, cache, gain, weight, q_out, picks, kv):
    heads_width = q_out.shape[1]
    first_head = idx[0] * 4
    row = iota((ROWS, ROWS), 0)
    turn = (local_row(row, 0, 0) == iota((ROWS, ROWS), 1)).astype(BF)
    normed = norm_rows(cache[...].astype(F32), gain[...])
    normed = dot(turn, normed).astype(BF)
    q_out[...] = dot_t(normed, weight[0:heads_width, :]).astype(BF).astype(F32)
    kv[...] = dot_t(normed, weight[heads_width:, :]).astype(BF).astype(F32)
    base = 0
    for level in range(BRANCHES):
        n = ROWS >> level
        column = iota((n, 2 * heads_width), 1)
        column = jnp.where(column >= heads_width, column - heads_width, column)
        got = jnp.zeros((n, 2 * heads_width), F32)
        for h in range(4):
            here = (column >= h * HDL) & (column < (h + 1) * HDL)
            got = jnp.where(here, kv[pl.ds(pick_start(first_head + h, level), n), :], got)
        if level == BRANCHES - 1:
            got = jnp.concatenate([got, jnp.zeros((8, 2 * heads_width), F32)], axis=0)
        picks[base : base + got.shape[0], :] = got.astype(BF)
        base += n


def slide_project(idx, cache, gain, weight):
    hw = weight.shape[0] // 3
    return pl.pallas_call(
        slide_kernel,
        out_shape=(
            jax.ShapeDtypeStruct((ROWS, hw), F32),
            jax.ShapeDtypeStruct((2 * ROWS, 2 * hw), BF),
        ),
        in_specs=[whole(pltpu.SMEM)] + [whole()] * 3,
        out_specs=(whole(),) * 2,
        scratch_shapes=[pltpu.VMEM((ROWS, 2 * hw), F32)],
        compiler_params=params(),
        name="slide_project",
    )(idx, cache, gain, weight)


def depth_of(x):
    return sum(((x & mask) == 0).astype(jnp.int32) for mask in (1, 3, 7, 15))


def attend_kernel(
    idx, *refs
):
    sources, (o0, o1, o2, o3), targets = refs[:5], refs[5:9], refs[9:14]
    q, peak, total, acc, sems = refs[14:]
    emb, q_cache, mine, theirs, out_w = targets
    loads = [
        pltpu.make_async_copy(source, target, sems.at[i])
        for i, (source, target) in enumerate(zip(sources, targets))
    ]
    for load in loads:
        load.start()
    mp, seq = idx[0], idx[1]
    first_head = mp * 4
    hw = q_cache.shape[1]
    scale = HDL ** (-0.5)
    slots = emb.shape[0]
    loads[0].wait()
    loads[1].wait()
    tail = emb[:, 3 * hw :]
    col = iota((8, tail.shape[1]), 1)
    digits = jnp.where(col == 0, 64.0, jnp.where(col == 1, 1.0, 0.0)).astype(BF)
    pos = dot_t(digits, tail).astype(jnp.int32)[0:1]
    spread = dot_t(tail, digits).astype(jnp.int32)[:, 0:1]
    own = seq * ROWS + local_row(iota((ROWS, 1), 0), 0, 0)
    match = own == pos
    found = jnp.max(match.astype(jnp.int32), axis=1, keepdims=True) > 0
    placed = dot(match.astype(BF), emb[:, 2 * hw : 3 * hw])
    q[...] = jnp.where(found, placed, q_cache[...])

    def head_mask(n, h):
        column = iota((n, hw), 1)
        return (column >= h * HDL) & (column < (h + 1) * HDL)

    def queries(level):
        n = ROWS >> level
        got = []
        for h in range(4):
            rows = q[...] if level == 0 else q[pl.ds(pick_start(first_head + h, level), n), :]
            got.append(jnp.where(head_mask(n, h), rows, 0.0))
        return jnp.concatenate(got, axis=0).astype(BF)

    full_q = queries(0)
    s = dot_t(full_q, emb[:, 0:hw]) * scale
    cross = (pos ^ (seq * ROWS)) >> 9
    first = sum(((cross >> b) != 0).astype(jnp.int32) for b in range(4))
    times = []
    for h in range(4):
        q_depth = depth_of(own ^ (first_head + h))
        k_depth = jnp.where(pos < 0, -1, depth_of(pos ^ (first_head + h)) - first)
        times.append(jnp.maximum(jnp.minimum(k_depth, q_depth - first) + 1, 0))
    times = jnp.concatenate(times, axis=0).astype(F32)
    s = jnp.where(times > 0.0, s, FLOOR_SCORE)
    m = jnp.max(s, axis=-1, keepdims=True)
    e = times * jnp.exp(s - m)
    peak[...] = jnp.broadcast_to(m, peak.shape)
    total[...] = jnp.broadcast_to(jnp.sum(e, axis=-1, keepdims=True), total.shape)
    acc[...] = dot(e.astype(BF), emb[:, hw : 2 * hw])

    loads[2].wait()
    loads[3].wait()
    for level in range(BRANCHES):
        n = ROWS >> level
        qb = full_q if level == 0 else queries(level)
        half = 512 if level == BRANCHES - 1 else 256
        low = BASES[level]
        last = level == BRANCHES - 1
        pitch = 16 if last else n
        turned = (rev4(spread & 15) << 3) + ((spread & 127) >> 4)
        cross_rows = (spread >> 7) ^ seq
        key = (cross_rows & 1) * half + (cross_rows >> 1) * pitch + (turned & (n - 1))
        inside = jnp.where((pos >= 0) & (first <= level), 1, 0)
        head_row = first_head + iota((8, slots), 0)
        hits = (((pos ^ head_row) & ((1 << level) - 1)) == 0) & (inside > 0)
        key_lane = iota((slots, 2 * half), 1)
        bias = dot(
            jnp.where(hits, FLOOR_SCORE, 0.0).astype(BF), (key_lane == key).astype(BF)
        )
        if last:
            bias = jnp.where((iota((8, 2 * half), 1) & 15) >= 8, FLOOR_SCORE, bias)
        sides = []
        for number, side in enumerate((mine, theirs)):
            s = dot_t(qb, side[low : low + half, 0:hw]) * scale
            flags = bias[0:4, number * half : (number + 1) * half]
            s = s.reshape(4, n, half) + flags[:, None, :]
            sides.append(s.reshape(4 * n, half))
        m = jnp.maximum(
            jnp.max(sides[0], axis=-1, keepdims=True), jnp.max(sides[1], axis=-1, keepdims=True)
        )
        e0, e1 = jnp.exp(sides[0] - m), jnp.exp(sides[1] - m)
        t = jnp.sum(e0, axis=-1, keepdims=True) + jnp.sum(e1, axis=-1, keepdims=True)
        o = dot(e0.astype(BF), mine[low : low + half, hw : 2 * hw]) + dot(
            e1.astype(BF), theirs[low : low + half, hw : 2 * hw]
        )
        for h in range(4):
            start = h * ROWS + (0 if level == 0 else pick_start(first_head + h, level))
            at = pl.ds(pl.multiple_of(start, 8), n)
            part = slice(h * n, (h + 1) * n)
            before = peak[at, :]
            after = jnp.maximum(before, m[part])
            keep, add = jnp.exp(before - after), jnp.exp(m[part] - after)
            peak[at, :] = after
            total[at, :] = total[at, :] * keep + t[part] * add
            acc[at, :] = acc[at, :] * keep[:, 0:1] + o[part] * add[:, 0:1]

    attended = jnp.zeros((ROWS, hw), F32)
    for h in range(4):
        rows = slice(h * ROWS, (h + 1) * ROWS)
        attended = jnp.where(head_mask(ROWS, h), acc[rows, :] / total[rows, 0:1], attended)
    turn = (local_row(iota((ROWS, ROWS), 1), 0, 0) == iota((ROWS, ROWS), 0)).astype(BF)
    attended = dot(turn, attended.astype(BF)).astype(BF)
    loads[4].wait()
    for d, o in enumerate((o0, o1, o2, o3)):
        o[...] = dot(attended, out_w[lax.rem(mp + d, 4)]).astype(BF)


def attend(idx, q_cache, mine, theirs, emb, out_w):
    hw = q_cache.shape[1]
    return pl.pallas_call(
        attend_kernel,
        out_shape=(jax.ShapeDtypeStruct((ROWS, hw), BF),) * 4,
        in_specs=[whole(pltpu.SMEM)] + [whole(pl.ANY)] * 5,
        out_specs=(whole(),) * 4,
        scratch_shapes=[pltpu.VMEM(x.shape, x.dtype) for x in (emb, q_cache, mine, theirs, out_w)]
        + [
            pltpu.VMEM((ROWS, hw), F32),
            pltpu.VMEM((4 * ROWS, 128), F32),
            pltpu.VMEM((4 * ROWS, 128), F32),
            pltpu.VMEM((4 * ROWS, hw), F32),
            pltpu.SemaphoreType.DMA((5,)),
        ],
        compiler_params=params(),
        name="attend",
    )(idx, emb, q_cache, mine, theirs, out_w)


def shift_mp(x, k):
    return lax.ppermute(x, "mp", [(i, (i + k) % 4) for i in range(4)])


def swap_seq(x, bit):
    return lax.ppermute(x, "seq", [(i, i ^ bit) for i in range(64)])


def local(
    tile_batch,
    positions,
    counts,
    vit_gain,
    vit_qkv,
    vit_out,
    tile_proj,
    seq_cache,
    long_gain,
    long_qkv,
    long_out,
):
    mp, seq = lax.axis_index("mp"), lax.axis_index("seq")
    idx = jnp.concatenate([jnp.stack([mp, seq]).astype(jnp.int32), counts, positions])
    slots, _, width = tile_batch.shape
    model = seq_cache.shape[1]
    hw = long_qkv.shape[-1]

    left, right = shift_mp(tile_batch, 1), shift_mp(tile_batch, 3)
    tile_w = vit_qkv.transpose(1, 0, 2)
    gain = vit_gain.reshape(1, 4 * width)

    slide_w = long_qkv.transpose(1, 2, 0).reshape(3 * hw, model)
    gain_row = long_gain.reshape(1, model)
    q_cache, picks = slide_project(idx, seq_cache, gain_row, slide_w)
    proj_here = lax.dynamic_slice_in_dim(tile_proj, mp * width, width, 0)
    joined = jnp.concatenate([dot(vit_out, tile_proj).astype(BF), proj_here], axis=0)
    far = [shift_mp(left[0:2], 1), shift_mp(right[2:4], 3)]

    kept = []

    def step(have, level):
        have = jnp.concatenate([have, swap_seq(have, 2 << level)], axis=0)
        if level == BRANCHES - 1:
            return have
        n = ROWS >> level
        kept.append(have[:, 0:n].reshape(-1, 2 * hw))
        return have[:, n:]

    have = step(step(step(picks[None], 0), 1), 2)
    far[0], have, joined = lax.optimization_barrier((far[0], have, joined))
    first = encode(idx, 0, tile_batch, left, right, far[0], gain, tile_w)
    have = step(have, 3)
    far[1], have, first = lax.optimization_barrier((far[1], have, first))
    second = encode(idx, 1, tile_batch, left, right, far[1], gain, tile_w)
    have = step(have, 4)
    mine = jnp.concatenate(kept + [have.reshape(-1, 2 * hw)], axis=0)
    first, second, mine = lax.optimization_barrier((first, second, mine))
    theirs = swap_seq(mine, 1)
    partial = dot(jnp.concatenate([first, second], axis=0).astype(BF), joined)
    shares = [partial] + [shift_mp(partial, k) for k in (1, 3, 2)]
    emb = embed_rows(idx, shares, gain_row, slide_w)
    emb = lax.all_to_all(jnp.broadcast_to(emb[None], (64,) + emb.shape), "seq", 0, 0)
    emb = emb.reshape(64 * slots, emb.shape[2])

    out_w = long_out.reshape(hw, 4, hw).transpose(1, 0, 2)
    o0, o1, o2, o3 = attend(idx, q_cache, mine, theirs, emb, out_w)
    terms = [o0, shift_mp(o1, 1), shift_mp(o2, 2), shift_mp(o3, 3)]
    a, b, c, d = [term.astype(F32) for term in terms]
    return ((a + b) + (c + d)).astype(BF)


def solution(mesh):
    placed = (
        P("seq", None, "mp"),
        P("seq"),
        P("seq"),
        P(),
        P(None, None, "mp"),
        P("mp", None),
        P(),
        P("seq", None),
        P(),
        P(None, None, "mp"),
        P("mp", None),
    )
    return jax.shard_map(
        local, mesh=mesh, in_specs=placed, out_specs=P("seq", "mp"), check_vma=False
    )
```

```python
import functools
import math

import jax
import jax.numpy as jnp
from jax import lax
from jax.experimental import pallas as pl
from jax.experimental.pallas import tpu as pltpu
from jax.sharding import PartitionSpec as P

HDT = 64
HDL = 48
BRANCHES = 5
EPSILON = 1e-05
FLOOR_SCORE = -1e30
BF = jnp.bfloat16
F32 = jnp.float32
ROWS = 128
BASES = (0, 256, 512, 768, 1024)


def params(mib=40):
    return pltpu.CompilerParams(vmem_limit_bytes=mib * 2**20)


def whole(kind=pltpu.VMEM):
    return pl.BlockSpec(memory_space=kind)


def dot(a, b):
    return jnp.dot(a, b, preferred_element_type=F32)


def dot_t(a, b):
    return lax.dot_general(a, b, (((1,), (1,)), ((), ())), preferred_element_type=F32)


def iota(shape, dim):
    return lax.broadcasted_iota(jnp.int32, shape, dim)


def encode_kernel(idx, own, left, right, far, gain, weight, out, xn, qk):
    mp = idx[0]
    tokens, width = own.shape[1], own.shape[2]
    unit = HDT ** (-0.5) * math.log2(math.e)
    features = 4 * width
    starts = [pl.multiple_of(lax.rem(mp + shift, 4) * width, 128) for shift in (0, 3, 1, 2)]
    for t in range(2):
        parts = [own[t], left[t], right[t], far[t]]
        wide = [part.astype(F32) for part in parts]
        total = sum(jnp.sum(part, axis=-1, keepdims=True) for part in wide)
        mean = total * (1.0 / features)
        centred = [part - mean for part in wide]
        spread = sum(jnp.sum(part * part, axis=-1, keepdims=True) for part in centred)
        scale = lax.rsqrt(spread * (1.0 / features) + EPSILON)
        for d in range(4):
            columns = pl.ds(starts[d], width)
            xn[t * tokens : (t + 1) * tokens, columns] = (
                centred[d] * scale * gain[:, columns]
            ).astype(BF)
        out[t : t + 1, width : 2 * width] = jnp.sum(wide[0], axis=0, keepdims=True) * (1.0 / tokens)
    for part in range(2):
        qk[:, part * width : (part + 1) * width] = dot(xn[...], weight[part]).astype(BF)
    lane = iota((tokens, 2 * HDT), 1)
    pooled = []
    for t in range(2):
        low, high = t * tokens, (t + 1) * tokens
        rows = []
        for pair in range(width // (2 * HDT)):
            q2 = qk[low:high, pair * 128 : (pair + 1) * 128]
            k2 = qk[low:high, width + pair * 128 : width + (pair + 1) * 128]
            for half in range(2):
                qm = jnp.where((lane >= HDT) == (half == 1), q2, jnp.zeros((), BF))
                s = dot_t(qm, k2)
                e = jnp.exp2((s - jnp.max(s, axis=-1, keepdims=True)) * unit)
                share = 1.0 / (jnp.sum(e, axis=-1, keepdims=True) * tokens)
                rows.append(jnp.sum(e * share, axis=0, keepdims=True))
        rows.append(jnp.zeros((8 - len(rows), tokens), F32))
        mix = jnp.concatenate(rows, axis=0).astype(BF)
        pooled.append(dot(mix, xn[low:high, :]))
    acc = dot(jnp.concatenate(pooled, axis=0).astype(BF), weight[2])
    keep = (iota((16, width), 0) & 7) == (iota((16, width), 1) >> 6)
    acc = jnp.where(keep, acc, 0.0)
    for t in range(2):
        out[t : t + 1, 0:width] = jnp.sum(acc[t * 8 : (t + 1) * 8], axis=0, keepdims=True)


def encode(idx, chunk, own, left, right, far, gain, weight):
    tokens, width = own.shape[1], own.shape[2]
    block = pl.BlockSpec((2, tokens, width), lambda i: (chunk, 0, 0))
    far_block = pl.BlockSpec((2, tokens, width), lambda i: (0, 0, 0))
    return pl.pallas_call(
        encode_kernel,
        grid=(1,),
        out_shape=jax.ShapeDtypeStruct((2, 2 * width), F32),
        in_specs=[whole(pltpu.SMEM), block, block, block, far_block, whole(), whole()],
        out_specs=whole(),
        scratch_shapes=[
            pltpu.VMEM((2 * tokens, 4 * width), BF),
            pltpu.VMEM((2 * tokens, 2 * width), BF),
        ],
        compiler_params=params(20),
        cost_estimate=pl.CostEstimate(
            flops=6 * 10**9, bytes_accessed=8 * 10**6, transcendentals=8 * 10**5
        ),
        name="encode",
    )(idx, own, left, right, far, gain, weight)


def norm_rows(x, gain):
    mean = jnp.mean(x, axis=-1, keepdims=True)
    centre = x - mean
    spread = jnp.mean(centre * centre, axis=-1, keepdims=True)
    return (centre * lax.rsqrt(spread + EPSILON) * gain).astype(BF)


def slot_digits(idx, slot):
    place = jnp.where(slot < idx[2], idx[3 + slot], -64)
    return (place >> 6).astype(F32), (place & 63).astype(F32)


def embed_kernel(idx, a, b, c, d, gain, weight, out):
    width = weight.shape[0]
    third = width // 3
    total = (a[...] + b[...]) + (c[...] + d[...])
    normed = norm_rows(total.astype(BF).astype(F32), gain[...])
    out[:, 0 : 2 * third] = dot_t(normed, weight[third:, :]).astype(BF)
    out[:, 2 * third : width] = dot_t(normed, weight[0:third, :]).astype(BF)
    shape = (out.shape[0], out.shape[1] - width)
    row, column = iota(shape, 0), iota(shape, 1)
    tail = jnp.zeros(shape, F32)
    for slot in range(shape[0]):
        high, low = slot_digits(idx, slot)
        tail = jnp.where((row == slot) & (column == 0), high, tail)
        tail = jnp.where((row == slot) & (column == 1), low, tail)
    out[:, width:] = tail.astype(BF)


def embed_rows(idx, parts, gain, weight):
    rows, width = parts[0].shape[0], weight.shape[0]
    return pl.pallas_call(
        embed_kernel,
        out_shape=jax.ShapeDtypeStruct((rows, width + 64), BF),
        in_specs=[whole(pltpu.SMEM)] + [whole()] * 6,
        out_specs=whole(),
        compiler_params=params(20),
        name="embed_rows",
    )(idx, *parts, gain, weight)


def rev4(x):
    return ((x & 1) << 3) | ((x & 2) << 1) | ((x & 4) >> 1) | ((x & 8) >> 3)


def pick_start(head, level):
    return pl.multiple_of((rev4(head & 15) >> (4 - level)) * (ROWS >> level), 8)


def local_row(j, level, head):
    bits = j >> 3
    free = 4 - level
    turned = rev4(bits) >> (4 - free) if free else bits * 0
    return (j & 7) * 16 + (turned << level) + (head & ((1 << level) - 1))


def slide_kernel(idx, cache, gain, weight, q_out, picks, kv):
    heads_width = q_out.shape[1]
    first_head = idx[0] * 4
    row = iota((ROWS, ROWS), 0)
    turn = (local_row(row, 0, 0) == iota((ROWS, ROWS), 1)).astype(BF)
    normed = norm_rows(cache[...].astype(F32), gain[...])
    normed = dot(turn, normed).astype(BF)
    q_out[...] = dot_t(normed, weight[0:heads_width, :]).astype(BF).astype(F32)
    kv[...] = dot_t(normed, weight[heads_width:, :]).astype(BF).astype(F32)
    base = 0
    for level in range(BRANCHES):
        n = ROWS >> level
        column = iota((n, 2 * heads_width), 1)
        column = jnp.where(column >= heads_width, column - heads_width, column)
        got = jnp.zeros((n, 2 * heads_width), F32)
        for h in range(4):
            here = (column >= h * HDL) & (column < (h + 1) * HDL)
            got = jnp.where(here, kv[pl.ds(pick_start(first_head + h, level), n), :], got)
        if level == BRANCHES - 1:
            got = jnp.concatenate([got, jnp.zeros((8, 2 * heads_width), F32)], axis=0)
        picks[base : base + got.shape[0], :] = got.astype(BF)
        base += n


def slide_project(idx, cache, gain, weight):
    hw = weight.shape[0] // 3
    return pl.pallas_call(
        slide_kernel,
        out_shape=(
            jax.ShapeDtypeStruct((ROWS, hw), F32),
            jax.ShapeDtypeStruct((2 * ROWS, 2 * hw), BF),
        ),
        in_specs=[whole(pltpu.SMEM)] + [whole()] * 3,
        out_specs=(whole(),) * 2,
        scratch_shapes=[pltpu.VMEM((ROWS, 2 * hw), F32)],
        compiler_params=params(20),
        name="slide_project",
    )(idx, cache, gain, weight)


def depth_of(x):
    return sum(((x & mask) == 0).astype(jnp.int32) for mask in (1, 3, 7, 15))


def attend_kernel(
    idx, *refs
):
    sources, (o0, o1, o2, o3), targets = refs[:5], refs[5:9], refs[9:14]
    q, peak, total, acc, sems = refs[14:]
    emb, q_cache, mine, theirs, out_w = targets
    loads = [
        pltpu.make_async_copy(source, target, sems.at[i])
        for i, (source, target) in enumerate(zip(sources, targets))
    ]
    for load in loads:
        load.start()
    mp, seq = idx[0], idx[1]
    first_head = mp * 4
    hw = q_cache.shape[1]
    scale = HDL ** (-0.5)
    slots = emb.shape[0]
    loads[0].wait()
    loads[1].wait()
    tail = emb[:, 3 * hw :]
    col = iota((8, tail.shape[1]), 1)
    digits = jnp.where(col == 0, 64.0, jnp.where(col == 1, 1.0, 0.0)).astype(BF)
    pos = dot_t(digits, tail).astype(jnp.int32)[0:1]
    spread = dot_t(tail, digits).astype(jnp.int32)[:, 0:1]
    own = seq * ROWS + local_row(iota((ROWS, 1), 0), 0, 0)
    match = own == pos
    found = jnp.max(match.astype(jnp.int32), axis=1, keepdims=True) > 0
    placed = dot(match.astype(BF), emb[:, 2 * hw : 3 * hw])
    q[...] = jnp.where(found, placed, q_cache[...])

    def head_mask(n, h):
        column = iota((n, hw), 1)
        return (column >= h * HDL) & (column < (h + 1) * HDL)

    def queries(level):
        n = ROWS >> level
        got = []
        for h in range(4):
            rows = q[...] if level == 0 else q[pl.ds(pick_start(first_head + h, level), n), :]
            got.append(jnp.where(head_mask(n, h), rows, 0.0))
        return jnp.concatenate(got, axis=0).astype(BF)

    full_q = queries(0)
    s = dot_t(full_q, emb[:, 0:hw]) * scale
    cross = (pos ^ (seq * ROWS)) >> 9
    first = sum(((cross >> b) != 0).astype(jnp.int32) for b in range(4))
    times = []
    for h in range(4):
        q_depth = depth_of(own ^ (first_head + h))
        k_depth = jnp.where(pos < 0, -1, depth_of(pos ^ (first_head + h)) - first)
        times.append(jnp.maximum(jnp.minimum(k_depth, q_depth - first) + 1, 0))
    times = jnp.concatenate(times, axis=0).astype(F32)
    s = jnp.where(times > 0.0, s, FLOOR_SCORE)
    m = jnp.max(s, axis=-1, keepdims=True)
    e = times * jnp.exp(s - m)
    peak[...] = jnp.broadcast_to(m, peak.shape)
    total[...] = jnp.broadcast_to(jnp.sum(e, axis=-1, keepdims=True), total.shape)
    acc[...] = dot(e.astype(BF), emb[:, hw : 2 * hw])

    loads[2].wait()
    loads[3].wait()
    for level in range(BRANCHES):
        n = ROWS >> level
        qb = full_q if level == 0 else queries(level)
        half = 512 if level == BRANCHES - 1 else 256
        low = BASES[level]
        last = level == BRANCHES - 1
        pitch = 16 if last else n
        turned = (rev4(spread & 15) << 3) + ((spread & 127) >> 4)
        cross_rows = (spread >> 7) ^ seq
        key = (cross_rows & 1) * half + (cross_rows >> 1) * pitch + (turned & (n - 1))
        inside = jnp.where((pos >= 0) & (first <= level), 1, 0)
        head_row = first_head + iota((8, slots), 0)
        hits = (((pos ^ head_row) & ((1 << level) - 1)) == 0) & (inside > 0)
        key_lane = iota((slots, 2 * half), 1)
        bias = dot(
            jnp.where(hits, FLOOR_SCORE, 0.0).astype(BF), (key_lane == key).astype(BF)
        )
        if last:
            bias = jnp.where((iota((8, 2 * half), 1) & 15) >= 8, FLOOR_SCORE, bias)
        sides = []
        for number, side in enumerate((mine, theirs)):
            s = dot_t(qb, side[low : low + half, 0:hw]) * scale
            flags = bias[0:4, number * half : (number + 1) * half]
            s = s.reshape(4, n, half) + flags[:, None, :]
            sides.append(s.reshape(4 * n, half))
        m = jnp.maximum(
            jnp.max(sides[0], axis=-1, keepdims=True), jnp.max(sides[1], axis=-1, keepdims=True)
        )
        e0, e1 = jnp.exp(sides[0] - m), jnp.exp(sides[1] - m)
        t = jnp.sum(e0, axis=-1, keepdims=True) + jnp.sum(e1, axis=-1, keepdims=True)
        o = dot(e0.astype(BF), mine[low : low + half, hw : 2 * hw]) + dot(
            e1.astype(BF), theirs[low : low + half, hw : 2 * hw]
        )
        for h in range(4):
            start = h * ROWS + (0 if level == 0 else pick_start(first_head + h, level))
            at = pl.ds(pl.multiple_of(start, 8), n)
            part = slice(h * n, (h + 1) * n)
            before = peak[at, :]
            after = jnp.maximum(before, m[part])
            keep, add = jnp.exp(before - after), jnp.exp(m[part] - after)
            peak[at, :] = after
            total[at, :] = total[at, :] * keep + t[part] * add
            acc[at, :] = acc[at, :] * keep[:, 0:1] + o[part] * add[:, 0:1]

    attended = jnp.zeros((ROWS, hw), F32)
    for h in range(4):
        rows = slice(h * ROWS, (h + 1) * ROWS)
        attended = jnp.where(head_mask(ROWS, h), acc[rows, :] / total[rows, 0:1], attended)
    turn = (local_row(iota((ROWS, ROWS), 1), 0, 0) == iota((ROWS, ROWS), 0)).astype(BF)
    attended = dot(turn, attended.astype(BF)).astype(BF)
    loads[4].wait()
    for d, o in enumerate((o0, o1, o2, o3)):
        o[...] = dot(attended, out_w[lax.rem(mp + d, 4)]).astype(BF)


def attend(idx, q_cache, mine, theirs, emb, out_w):
    hw = q_cache.shape[1]
    return pl.pallas_call(
        attend_kernel,
        out_shape=(jax.ShapeDtypeStruct((ROWS, hw), BF),) * 4,
        in_specs=[whole(pltpu.SMEM)] + [whole(pltpu.HBM)] * 5,
        out_specs=(whole(),) * 4,
        scratch_shapes=[pltpu.VMEM(x.shape, x.dtype) for x in (emb, q_cache, mine, theirs, out_w)]
        + [
            pltpu.VMEM((ROWS, hw), F32),
            pltpu.VMEM((4 * ROWS, 128), F32),
            pltpu.VMEM((4 * ROWS, 128), F32),
            pltpu.VMEM((4 * ROWS, hw), F32),
            pltpu.SemaphoreType.DMA((5,)),
        ],
        compiler_params=params(20),
        name="attend",
    )(idx, emb, q_cache, mine, theirs, out_w)


def shift_mp(x, k):
    return lax.ppermute(x, "mp", [(i, (i + k) % 4) for i in range(4)])


def swap_seq(x, bit):
    return lax.ppermute(x, "seq", [(i, i ^ bit) for i in range(64)])


def local(
    tile_batch,
    positions,
    counts,
    vit_gain,
    vit_qkv,
    vit_out,
    tile_proj,
    seq_cache,
    long_gain,
    long_qkv,
    long_out,
):
    mp, seq = lax.axis_index("mp"), lax.axis_index("seq")
    idx = jnp.concatenate([jnp.stack([mp, seq]).astype(jnp.int32), counts, positions])
    slots, _, width = tile_batch.shape
    model = seq_cache.shape[1]
    hw = long_qkv.shape[-1]

    left, right = shift_mp(tile_batch, 1), shift_mp(tile_batch, 3)
    tile_w = vit_qkv.transpose(1, 0, 2)
    gain = vit_gain.reshape(1, 4 * width)

    slide_w = long_qkv.transpose(1, 2, 0).reshape(3 * hw, model)
    gain_row = long_gain.reshape(1, model)
    q_cache, picks = slide_project(idx, seq_cache, gain_row, slide_w)
    proj_here = lax.dynamic_slice_in_dim(tile_proj, mp * width, width, 0)
    joined = jnp.concatenate([dot(vit_out, tile_proj).astype(BF), proj_here], axis=0)
    far = [shift_mp(left[0:2], 1), shift_mp(right[2:4], 3)]

    kept = []

    def step(have, level):
        have = jnp.concatenate([have, swap_seq(have, 2 << level)], axis=0)
        if level == BRANCHES - 1:
            return have
        n = ROWS >> level
        kept.append(have[:, 0:n].reshape(-1, 2 * hw))
        return have[:, n:]

    have = step(step(picks[None], 0), 1)
    far[0], have, joined = lax.optimization_barrier((far[0], have, joined))
    first = encode(idx, 0, tile_batch, left, right, far[0], gain, tile_w)
    have = step(have, 2)
    far[1], have, first = lax.optimization_barrier((far[1], have, first))
    second = encode(idx, 1, tile_batch, left, right, far[1], gain, tile_w)
    have = step(have, 3)
    first, second, have = lax.optimization_barrier((first, second, have))
    partial = dot(jnp.concatenate([first, second], axis=0).astype(BF), joined)
    shares = [partial] + [shift_mp(partial, k) for k in (1, 3, 2)]
    have = step(have, 4)
    mine = jnp.concatenate(kept + [have.reshape(-1, 2 * hw)], axis=0)
    shares, mine = lax.optimization_barrier((shares, mine))
    theirs = swap_seq(mine, 1)
    emb = embed_rows(idx, shares, gain_row, slide_w)
    emb = lax.all_to_all(jnp.broadcast_to(emb[None], (64,) + emb.shape), "seq", 0, 0)
    emb = emb.reshape(64 * slots, emb.shape[2])

    out_w = long_out.reshape(hw, 4, hw).transpose(1, 0, 2)
    o0, o1, o2, o3 = attend(idx, q_cache, mine, theirs, emb, out_w)
    terms = [o0, shift_mp(o1, 1), shift_mp(o2, 2), shift_mp(o3, 3)]
    a, b, c, d = [term.astype(F32) for term in terms]
    return ((a + b) + (c + d)).astype(BF)


def solution(mesh):
    placed = (
        P("seq", None, "mp"),
        P("seq"),
        P("seq"),
        P(),
        P(None, None, "mp"),
        P("mp", None),
        P(),
        P("seq", None),
        P(),
        P(None, None, "mp"),
        P("mp", None),
    )
    return jax.shard_map(
        local, mesh=mesh, in_specs=placed, out_specs=P("seq", "mp"), check_vma=False
    )
```

```python
import functools
import math

import jax
import jax.numpy as jnp
from jax import lax
from jax.experimental import pallas as pl
from jax.experimental.pallas import tpu as pltpu
from jax.sharding import PartitionSpec as P

HDT = 64
HDL = 48
BRANCHES = 5
EPSILON = 1e-05
FLOOR_SCORE = -1e30
BF = jnp.bfloat16
F32 = jnp.float32
ROWS = 128
BASES = (0, 256, 512, 768, 1024)


def params(mib=40):
    return pltpu.CompilerParams(vmem_limit_bytes=mib * 2**20)


def whole(kind=pltpu.VMEM):
    return pl.BlockSpec(memory_space=kind)


def dot(a, b):
    return jnp.dot(a, b, preferred_element_type=F32)


def dot_t(a, b):
    return lax.dot_general(a, b, (((1,), (1,)), ((), ())), preferred_element_type=F32)


def iota(shape, dim):
    return lax.broadcasted_iota(jnp.int32, shape, dim)


def encode_kernel(idx, own, left, right, far, gain, weight, out, xn, qk):
    mp = idx[0]
    tokens, width = own.shape[1], own.shape[2]
    unit = HDT ** (-0.5) * math.log2(math.e)
    features = 4 * width
    starts = [pl.multiple_of(lax.rem(mp + shift, 4) * width, 128) for shift in (0, 3, 1, 2)]
    for t in range(2):
        parts = [own[t], left[t], right[t], far[t]]
        wide = [part.astype(F32) for part in parts]
        total = sum(jnp.sum(part, axis=-1, keepdims=True) for part in wide)
        mean = total * (1.0 / features)
        centred = [part - mean for part in wide]
        spread = sum(jnp.sum(part * part, axis=-1, keepdims=True) for part in centred)
        scale = lax.rsqrt(spread * (1.0 / features) + EPSILON)
        for d in range(4):
            columns = pl.ds(starts[d], width)
            xn[t * tokens : (t + 1) * tokens, columns] = (
                centred[d] * scale * gain[:, columns]
            ).astype(BF)
        out[t : t + 1, width : 2 * width] = jnp.sum(wide[0], axis=0, keepdims=True) * (1.0 / tokens)
    for part in range(2):
        qk[:, part * width : (part + 1) * width] = dot(xn[...], weight[part]).astype(BF)
    lane = iota((tokens, 2 * HDT), 1)
    pooled = []
    for t in range(2):
        low, high = t * tokens, (t + 1) * tokens
        rows = []
        for pair in range(width // (2 * HDT)):
            q2 = qk[low:high, pair * 128 : (pair + 1) * 128]
            k2 = qk[low:high, width + pair * 128 : width + (pair + 1) * 128]
            for half in range(2):
                qm = jnp.where((lane >= HDT) == (half == 1), q2, jnp.zeros((), BF))
                s = dot_t(qm, k2)
                e = jnp.exp2((s - jnp.max(s, axis=-1, keepdims=True)) * unit)
                share = 1.0 / (jnp.sum(e, axis=-1, keepdims=True) * tokens)
                rows.append(jnp.sum(e * share, axis=0, keepdims=True))
        rows.append(jnp.zeros((8 - len(rows), tokens), F32))
        mix = jnp.concatenate(rows, axis=0).astype(BF)
        pooled.append(dot(mix, xn[low:high, :]))
    acc = dot(jnp.concatenate(pooled, axis=0).astype(BF), weight[2])
    keep = (iota((16, width), 0) & 7) == (iota((16, width), 1) >> 6)
    acc = jnp.where(keep, acc, 0.0)
    for t in range(2):
        out[t : t + 1, 0:width] = jnp.sum(acc[t * 8 : (t + 1) * 8], axis=0, keepdims=True)


def encode(idx, chunk, own, left, right, far, gain, weight):
    tokens, width = own.shape[1], own.shape[2]
    block = pl.BlockSpec((2, tokens, width), lambda i: (chunk, 0, 0))
    far_block = pl.BlockSpec((2, tokens, width), lambda i: (0, 0, 0))
    return pl.pallas_call(
        encode_kernel,
        grid=(1,),
        out_shape=jax.ShapeDtypeStruct((2, 2 * width), F32),
        in_specs=[whole(pltpu.SMEM), block, block, block, far_block, whole(), whole()],
        out_specs=whole(),
        scratch_shapes=[
            pltpu.VMEM((2 * tokens, 4 * width), BF),
            pltpu.VMEM((2 * tokens, 2 * width), BF),
        ],
        compiler_params=params(20),
        cost_estimate=pl.CostEstimate(
            flops=6 * 10**9, bytes_accessed=8 * 10**6, transcendentals=8 * 10**5
        ),
        name="encode",
    )(idx, own, left, right, far, gain, weight)


def norm_rows(x, gain):
    mean = jnp.mean(x, axis=-1, keepdims=True)
    centre = x - mean
    spread = jnp.mean(centre * centre, axis=-1, keepdims=True)
    return (centre * lax.rsqrt(spread + EPSILON) * gain).astype(BF)


def slot_digits(idx, slot):
    place = jnp.where(slot < idx[2], idx[3 + slot], -64)
    return (place >> 6).astype(F32), (place & 63).astype(F32)


def embed_kernel(idx, a, b, c, d, gain, weight, out):
    width = weight.shape[0]
    third = width // 3
    total = (a[...] + b[...]) + (c[...] + d[...])
    normed = norm_rows(total.astype(BF).astype(F32), gain[...])
    out[:, 0 : 2 * third] = dot_t(normed, weight[third:, :]).astype(BF)
    out[:, 2 * third : width] = dot_t(normed, weight[0:third, :]).astype(BF)
    shape = (out.shape[0], out.shape[1] - width)
    row, column = iota(shape, 0), iota(shape, 1)
    tail = jnp.zeros(shape, F32)
    for slot in range(shape[0]):
        high, low = slot_digits(idx, slot)
        tail = jnp.where((row == slot) & (column == 0), high, tail)
        tail = jnp.where((row == slot) & (column == 1), low, tail)
    out[:, width:] = tail.astype(BF)


def embed_rows(idx, parts, gain, weight):
    rows, width = parts[0].shape[0], weight.shape[0]
    return pl.pallas_call(
        embed_kernel,
        out_shape=jax.ShapeDtypeStruct((rows, width + 64), BF),
        in_specs=[whole(pltpu.SMEM)] + [whole()] * 6,
        out_specs=whole(),
        compiler_params=params(20),
        name="embed_rows",
    )(idx, *parts, gain, weight)


def rev4(x):
    return ((x & 1) << 3) | ((x & 2) << 1) | ((x & 4) >> 1) | ((x & 8) >> 3)


def pick_start(head, level):
    return pl.multiple_of((rev4(head & 15) >> (4 - level)) * (ROWS >> level), 8)


def local_row(j, level, head):
    bits = j >> 3
    free = 4 - level
    turned = rev4(bits) >> (4 - free) if free else bits * 0
    return (j & 7) * 16 + (turned << level) + (head & ((1 << level) - 1))


def slide_kernel(idx, cache, gain, weight, q_out, picks, kv):
    heads_width = q_out.shape[1]
    first_head = idx[0] * 4
    row = iota((ROWS, ROWS), 0)
    turn = (local_row(row, 0, 0) == iota((ROWS, ROWS), 1)).astype(BF)
    normed = norm_rows(cache[...].astype(F32), gain[...])
    normed = dot(turn, normed).astype(BF)
    q_out[...] = dot_t(normed, weight[0:heads_width, :]).astype(BF).astype(F32)
    kv[...] = dot_t(normed, weight[heads_width:, :]).astype(BF).astype(F32)
    base = 0
    for level in range(BRANCHES):
        n = ROWS >> level
        column = iota((n, 2 * heads_width), 1)
        column = jnp.where(column >= heads_width, column - heads_width, column)
        got = jnp.zeros((n, 2 * heads_width), F32)
        for h in range(4):
            here = (column >= h * HDL) & (column < (h + 1) * HDL)
            got = jnp.where(here, kv[pl.ds(pick_start(first_head + h, level), n), :], got)
        if level == BRANCHES - 1:
            got = jnp.concatenate([got, jnp.zeros((8, 2 * heads_width), F32)], axis=0)
        picks[base : base + got.shape[0], :] = got.astype(BF)
        base += n


def slide_project(idx, cache, gain, weight):
    hw = weight.shape[0] // 3
    return pl.pallas_call(
        slide_kernel,
        out_shape=(
            jax.ShapeDtypeStruct((ROWS, hw), F32),
            jax.ShapeDtypeStruct((2 * ROWS, 2 * hw), BF),
        ),
        in_specs=[whole(pltpu.SMEM)] + [whole()] * 3,
        out_specs=(whole(),) * 2,
        scratch_shapes=[pltpu.VMEM((ROWS, 2 * hw), F32)],
        compiler_params=params(20),
        name="slide_project",
    )(idx, cache, gain, weight)


def depth_of(x):
    return sum(((x & mask) == 0).astype(jnp.int32) for mask in (1, 3, 7, 15))


def attend_kernel(
    idx, *refs
):
    sources, (o0, o1, o2, o3), targets = refs[:5], refs[5:9], refs[9:14]
    q, peak, total, acc, sems = refs[14:]
    emb, q_cache, mine, theirs, out_w = targets
    loads = [
        pltpu.make_async_copy(source, target, sems.at[i])
        for i, (source, target) in enumerate(zip(sources, targets))
    ]
    for load in loads:
        load.start()
    mp, seq = idx[0], idx[1]
    first_head = mp * 4
    hw = q_cache.shape[1]
    scale = HDL ** (-0.5)
    slots = emb.shape[0]
    loads[0].wait()
    loads[1].wait()
    tail = emb[:, 3 * hw :]
    col = iota((8, tail.shape[1]), 1)
    digits = jnp.where(col == 0, 64.0, jnp.where(col == 1, 1.0, 0.0)).astype(BF)
    pos = dot_t(digits, tail).astype(jnp.int32)[0:1]
    spread = dot_t(tail, digits).astype(jnp.int32)[:, 0:1]
    own = seq * ROWS + local_row(iota((ROWS, 1), 0), 0, 0)
    match = own == pos
    found = jnp.max(match.astype(jnp.int32), axis=1, keepdims=True) > 0
    placed = dot(match.astype(BF), emb[:, 2 * hw : 3 * hw])
    q[...] = jnp.where(found, placed, q_cache[...])

    def head_mask(n, h):
        column = iota((n, hw), 1)
        return (column >= h * HDL) & (column < (h + 1) * HDL)

    def queries(level):
        n = ROWS >> level
        got = []
        for h in range(4):
            rows = q[...] if level == 0 else q[pl.ds(pick_start(first_head + h, level), n), :]
            got.append(jnp.where(head_mask(n, h), rows, 0.0))
        return jnp.concatenate(got, axis=0).astype(BF)

    full_q = queries(0)
    s = dot_t(full_q, emb[:, 0:hw]) * scale
    cross = (pos ^ (seq * ROWS)) >> 9
    first = sum(((cross >> b) != 0).astype(jnp.int32) for b in range(4))
    times = []
    for h in range(4):
        q_depth = depth_of(own ^ (first_head + h))
        k_depth = jnp.where(pos < 0, -1, depth_of(pos ^ (first_head + h)) - first)
        times.append(jnp.maximum(jnp.minimum(k_depth, q_depth - first) + 1, 0))
    times = jnp.concatenate(times, axis=0).astype(F32)
    s = jnp.where(times > 0.0, s, FLOOR_SCORE)
    m = jnp.max(s, axis=-1, keepdims=True)
    e = times * jnp.exp(s - m)
    peak[...] = jnp.broadcast_to(m, peak.shape)
    total[...] = jnp.broadcast_to(jnp.sum(e, axis=-1, keepdims=True), total.shape)
    acc[...] = dot(e.astype(BF), emb[:, hw : 2 * hw])

    loads[2].wait()
    loads[3].wait()
    for level in range(BRANCHES):
        n = ROWS >> level
        qb = full_q if level == 0 else queries(level)
        half = 512 if level == BRANCHES - 1 else 256
        low = BASES[level]
        last = level == BRANCHES - 1
        pitch = 16 if last else n
        turned = (rev4(spread & 15) << 3) + ((spread & 127) >> 4)
        cross_rows = (spread >> 7) ^ seq
        key = (cross_rows & 1) * half + (cross_rows >> 1) * pitch + (turned & (n - 1))
        inside = jnp.where((pos >= 0) & (first <= level), 1, 0)
        head_row = first_head + iota((8, slots), 0)
        hits = (((pos ^ head_row) & ((1 << level) - 1)) == 0) & (inside > 0)
        key_lane = iota((slots, 2 * half), 1)
        bias = dot(
            jnp.where(hits, FLOOR_SCORE, 0.0).astype(BF), (key_lane == key).astype(BF)
        )
        if last:
            bias = jnp.where((iota((8, 2 * half), 1) & 15) >= 8, FLOOR_SCORE, bias)
        sides = []
        for number, side in enumerate((mine, theirs)):
            s = dot_t(qb, side[low : low + half, 0:hw]) * scale
            flags = bias[0:4, number * half : (number + 1) * half]
            s = s.reshape(4, n, half) + flags[:, None, :]
            sides.append(s.reshape(4 * n, half))
        m = jnp.maximum(
            jnp.max(sides[0], axis=-1, keepdims=True), jnp.max(sides[1], axis=-1, keepdims=True)
        )
        e0, e1 = jnp.exp(sides[0] - m), jnp.exp(sides[1] - m)
        t = jnp.sum(e0, axis=-1, keepdims=True) + jnp.sum(e1, axis=-1, keepdims=True)
        o = dot(e0.astype(BF), mine[low : low + half, hw : 2 * hw]) + dot(
            e1.astype(BF), theirs[low : low + half, hw : 2 * hw]
        )
        for h in range(4):
            start = h * ROWS + (0 if level == 0 else pick_start(first_head + h, level))
            at = pl.ds(pl.multiple_of(start, 8), n)
            part = slice(h * n, (h + 1) * n)
            before = peak[at, :]
            after = jnp.maximum(before, m[part])
            keep, add = jnp.exp(before - after), jnp.exp(m[part] - after)
            peak[at, :] = after
            total[at, :] = total[at, :] * keep + t[part] * add
            acc[at, :] = acc[at, :] * keep[:, 0:1] + o[part] * add[:, 0:1]

    attended = jnp.zeros((ROWS, hw), F32)
    for h in range(4):
        rows = slice(h * ROWS, (h + 1) * ROWS)
        attended = jnp.where(head_mask(ROWS, h), acc[rows, :] / total[rows, 0:1], attended)
    turn = (local_row(iota((ROWS, ROWS), 1), 0, 0) == iota((ROWS, ROWS), 0)).astype(BF)
    attended = dot(turn, attended.astype(BF)).astype(BF)
    loads[4].wait()
    for d, o in enumerate((o0, o1, o2, o3)):
        o[...] = dot(attended, out_w[lax.rem(mp + d, 4)]).astype(BF)


def attend(idx, q_cache, mine, theirs, emb, out_w):
    hw = q_cache.shape[1]
    return pl.pallas_call(
        attend_kernel,
        out_shape=(jax.ShapeDtypeStruct((ROWS, hw), BF),) * 4,
        in_specs=[whole(pltpu.SMEM)] + [whole(pltpu.HBM)] * 5,
        out_specs=(whole(),) * 4,
        scratch_shapes=[pltpu.VMEM(x.shape, x.dtype) for x in (emb, q_cache, mine, theirs, out_w)]
        + [
            pltpu.VMEM((ROWS, hw), F32),
            pltpu.VMEM((4 * ROWS, 128), F32),
            pltpu.VMEM((4 * ROWS, 128), F32),
            pltpu.VMEM((4 * ROWS, hw), F32),
            pltpu.SemaphoreType.DMA((5,)),
        ],
        compiler_params=params(60),
        name="attend",
    )(idx, emb, q_cache, mine, theirs, out_w)


def shift_mp(x, k):
    return lax.ppermute(x, "mp", [(i, (i + k) % 4) for i in range(4)])


def swap_seq(x, bit):
    return lax.ppermute(x, "seq", [(i, i ^ bit) for i in range(64)])


def local(
    tile_batch,
    positions,
    counts,
    vit_gain,
    vit_qkv,
    vit_out,
    tile_proj,
    seq_cache,
    long_gain,
    long_qkv,
    long_out,
):
    mp, seq = lax.axis_index("mp"), lax.axis_index("seq")
    idx = jnp.concatenate([jnp.stack([mp, seq]).astype(jnp.int32), counts, positions])
    slots, _, width = tile_batch.shape
    model = seq_cache.shape[1]
    hw = long_qkv.shape[-1]

    left, right = shift_mp(tile_batch, 1), shift_mp(tile_batch, 3)
    tile_w = vit_qkv.transpose(1, 0, 2)
    gain = vit_gain.reshape(1, 4 * width)

    slide_w = long_qkv.transpose(1, 2, 0).reshape(3 * hw, model)
    gain_row = long_gain.reshape(1, model)
    q_cache, picks = slide_project(idx, seq_cache, gain_row, slide_w)
    proj_here = lax.dynamic_slice_in_dim(tile_proj, mp * width, width, 0)
    joined = jnp.concatenate([dot(vit_out, tile_proj).astype(BF), proj_here], axis=0)
    far = [shift_mp(left[0:2], 1), shift_mp(right[2:4], 3)]

    kept = []

    def step(have, level):
        have = jnp.concatenate([have, swap_seq(have, 2 << level)], axis=0)
        if level == BRANCHES - 1:
            return have
        n = ROWS >> level
        kept.append(have[:, 0:n].reshape(-1, 2 * hw))
        return have[:, n:]

    have = step(step(picks[None], 0), 1)
    far[0], have, joined = lax.optimization_barrier((far[0], have, joined))
    first = encode(idx, 0, tile_batch, left, right, far[0], gain, tile_w)
    have = step(have, 2)
    far[1], first = lax.optimization_barrier((far[1], first))
    second = encode(idx, 1, tile_batch, left, right, far[1], gain, tile_w)
    first, second, have = lax.optimization_barrier((first, second, have))
    partial = dot(jnp.concatenate([first, second], axis=0).astype(BF), joined)
    shares = [partial] + [shift_mp(partial, k) for k in (1, 3, 2)]
    have = step(have, 3)
    shares, have = lax.optimization_barrier((shares, have))
    have = step(have, 4)
    mine = jnp.concatenate(kept + [have.reshape(-1, 2 * hw)], axis=0)
    theirs = swap_seq(mine, 1)
    emb = embed_rows(idx, shares, gain_row, slide_w)
    emb = lax.all_to_all(jnp.broadcast_to(emb[None], (64,) + emb.shape), "seq", 0, 0)
    emb = emb.reshape(64 * slots, emb.shape[2])

    out_w = long_out.reshape(hw, 4, hw).transpose(1, 0, 2)
    o0, o1, o2, o3 = attend(idx, q_cache, mine, theirs, emb, out_w)
    terms = [o0, shift_mp(o1, 1), shift_mp(o2, 2), shift_mp(o3, 3)]
    a, b, c, d = [term.astype(F32) for term in terms]
    return ((a + b) + (c + d)).astype(BF)


def solution(mesh):
    placed = (
        P("seq", None, "mp"),
        P("seq"),
        P("seq"),
        P(),
        P(None, None, "mp"),
        P("mp", None),
        P(),
        P("seq", None),
        P(),
        P(None, None, "mp"),
        P("mp", None),
    )
    return jax.shard_map(
        local, mesh=mesh, in_specs=placed, out_specs=P("seq", "mp"), check_vma=False
    )
```

```python
import functools
import math

import jax
import jax.numpy as jnp
from jax import lax
from jax.experimental import pallas as pl
from jax.experimental.pallas import tpu as pltpu
from jax.sharding import PartitionSpec as P

HDT = 64
HDL = 48
BRANCHES = 5
EPSILON = 1e-05
FLOOR_SCORE = -1e30
BF = jnp.bfloat16
F32 = jnp.float32
ROWS = 128
BASES = (0, 256, 512, 768, 1024)


def params(mib=40):
    return pltpu.CompilerParams(vmem_limit_bytes=mib * 2**20)


def whole(kind=pltpu.VMEM):
    return pl.BlockSpec(memory_space=kind)


def dot(a, b):
    return jnp.dot(a, b, preferred_element_type=F32)


def dot_t(a, b):
    return lax.dot_general(a, b, (((1,), (1,)), ((), ())), preferred_element_type=F32)


def iota(shape, dim):
    return lax.broadcasted_iota(jnp.int32, shape, dim)


def encode_kernel(idx, own, left, right, far, gain, weight, out, xn, qk):
    mp = idx[0]
    tokens, width = own.shape[1], own.shape[2]
    unit = HDT ** (-0.5) * math.log2(math.e)
    features = 4 * width
    starts = [pl.multiple_of(lax.rem(mp + shift, 4) * width, 128) for shift in (0, 3, 1, 2)]
    for t in range(2):
        parts = [own[t], left[t], right[t], far[t]]
        wide = [part.astype(F32) for part in parts]
        total = sum(jnp.sum(part, axis=-1, keepdims=True) for part in wide)
        mean = total * (1.0 / features)
        centred = [part - mean for part in wide]
        spread = sum(jnp.sum(part * part, axis=-1, keepdims=True) for part in centred)
        scale = lax.rsqrt(spread * (1.0 / features) + EPSILON)
        for d in range(4):
            columns = pl.ds(starts[d], width)
            xn[t * tokens : (t + 1) * tokens, columns] = (
                centred[d] * scale * gain[:, columns]
            ).astype(BF)
        out[t : t + 1, width : 2 * width] = jnp.sum(wide[0], axis=0, keepdims=True) * (1.0 / tokens)
    for part in range(2):
        qk[:, part * width : (part + 1) * width] = dot(xn[...], weight[part]).astype(BF)
    lane = iota((tokens, 2 * HDT), 1)
    pooled = []
    for t in range(2):
        low, high = t * tokens, (t + 1) * tokens
        rows = []
        for pair in range(width // (2 * HDT)):
            q2 = qk[low:high, pair * 128 : (pair + 1) * 128]
            k2 = qk[low:high, width + pair * 128 : width + (pair + 1) * 128]
            for half in range(2):
                qm = jnp.where((lane >= HDT) == (half == 1), q2, jnp.zeros((), BF))
                s = dot_t(qm, k2)
                e = jnp.exp2((s - jnp.max(s, axis=-1, keepdims=True)) * unit)
                share = 1.0 / (jnp.sum(e, axis=-1, keepdims=True) * tokens)
                rows.append(jnp.sum(e * share, axis=0, keepdims=True))
        rows.append(jnp.zeros((8 - len(rows), tokens), F32))
        mix = jnp.concatenate(rows, axis=0).astype(BF)
        pooled.append(dot(mix, xn[low:high, :]))
    acc = dot(jnp.concatenate(pooled, axis=0).astype(BF), weight[2])
    keep = (iota((16, width), 0) & 7) == (iota((16, width), 1) >> 6)
    acc = jnp.where(keep, acc, 0.0)
    for t in range(2):
        out[t : t + 1, 0:width] = jnp.sum(acc[t * 8 : (t + 1) * 8], axis=0, keepdims=True)


def encode(idx, chunk, own, left, right, far, gain, weight):
    tokens, width = own.shape[1], own.shape[2]
    block = pl.BlockSpec((2, tokens, width), lambda i: (chunk, 0, 0))
    far_block = pl.BlockSpec((2, tokens, width), lambda i: (0, 0, 0))
    return pl.pallas_call(
        encode_kernel,
        grid=(1,),
        out_shape=jax.ShapeDtypeStruct((2, 2 * width), F32),
        in_specs=[whole(pltpu.SMEM), block, block, block, far_block, whole(), whole()],
        out_specs=whole(),
        scratch_shapes=[
            pltpu.VMEM((2 * tokens, 4 * width), BF),
            pltpu.VMEM((2 * tokens, 2 * width), BF),
        ],
        compiler_params=params(20),
        cost_estimate=pl.CostEstimate(
            flops=6 * 10**9, bytes_accessed=8 * 10**6, transcendentals=8 * 10**5
        ),
        name="encode",
    )(idx, own, left, right, far, gain, weight)


def norm_rows(x, gain):
    mean = jnp.mean(x, axis=-1, keepdims=True)
    centre = x - mean
    spread = jnp.mean(centre * centre, axis=-1, keepdims=True)
    return (centre * lax.rsqrt(spread + EPSILON) * gain).astype(BF)


def slot_digits(idx, slot):
    place = jnp.where(slot < idx[2], idx[3 + slot], -64)
    return (place >> 6).astype(F32), (place & 63).astype(F32)


def embed_kernel(idx, a, b, c, d, gain, weight, out):
    width = weight.shape[0]
    third = width // 3
    total = (a[...] + b[...]) + (c[...] + d[...])
    normed = norm_rows(total.astype(BF).astype(F32), gain[...])
    out[:, 0 : 2 * third] = dot_t(normed, weight[third:, :]).astype(BF)
    out[:, 2 * third : width] = dot_t(normed, weight[0:third, :]).astype(BF)
    shape = (out.shape[0], out.shape[1] - width)
    row, column = iota(shape, 0), iota(shape, 1)
    tail = jnp.zeros(shape, F32)
    for slot in range(shape[0]):
        high, low = slot_digits(idx, slot)
        tail = jnp.where((row == slot) & (column == 0), high, tail)
        tail = jnp.where((row == slot) & (column == 1), low, tail)
    out[:, width:] = tail.astype(BF)


def embed_rows(idx, parts, gain, weight):
    rows, width = parts[0].shape[0], weight.shape[0]
    return pl.pallas_call(
        embed_kernel,
        out_shape=jax.ShapeDtypeStruct((rows, width + 64), BF),
        in_specs=[whole(pltpu.SMEM)] + [whole()] * 6,
        out_specs=whole(),
        compiler_params=params(20),
        name="embed_rows",
    )(idx, *parts, gain, weight)


def rev4(x):
    return ((x & 1) << 3) | ((x & 2) << 1) | ((x & 4) >> 1) | ((x & 8) >> 3)


def pick_start(head, level):
    return pl.multiple_of((rev4(head & 15) >> (4 - level)) * (ROWS >> level), 8)


def local_row(j, level, head):
    bits = j >> 3
    free = 4 - level
    turned = rev4(bits) >> (4 - free) if free else bits * 0
    return (j & 7) * 16 + (turned << level) + (head & ((1 << level) - 1))


def slide_kernel(idx, cache, gain, weight, q_out, picks, kv):
    heads_width = q_out.shape[1]
    first_head = idx[0] * 4
    row = iota((ROWS, ROWS), 0)
    turn = (local_row(row, 0, 0) == iota((ROWS, ROWS), 1)).astype(BF)
    normed = norm_rows(cache[...].astype(F32), gain[...])
    normed = dot(turn, normed).astype(BF)
    q_out[...] = dot_t(normed, weight[0:heads_width, :]).astype(BF).astype(F32)
    kv[...] = dot_t(normed, weight[heads_width:, :]).astype(BF).astype(F32)
    base = 0
    for level in range(BRANCHES):
        n = ROWS >> level
        column = iota((n, 2 * heads_width), 1)
        column = jnp.where(column >= heads_width, column - heads_width, column)
        got = jnp.zeros((n, 2 * heads_width), F32)
        for h in range(4):
            here = (column >= h * HDL) & (column < (h + 1) * HDL)
            got = jnp.where(here, kv[pl.ds(pick_start(first_head + h, level), n), :], got)
        if level == BRANCHES - 1:
            got = jnp.concatenate([got, jnp.zeros((8, 2 * heads_width), F32)], axis=0)
        picks[base : base + got.shape[0], :] = got.astype(BF)
        base += n


def slide_project(idx, cache, gain, weight):
    hw = weight.shape[0] // 3
    return pl.pallas_call(
        slide_kernel,
        out_shape=(
            jax.ShapeDtypeStruct((ROWS, hw), F32),
            jax.ShapeDtypeStruct((2 * ROWS, 2 * hw), BF),
        ),
        in_specs=[whole(pltpu.SMEM)] + [whole()] * 3,
        out_specs=(whole(),) * 2,
        scratch_shapes=[pltpu.VMEM((ROWS, 2 * hw), F32)],
        compiler_params=params(20),
        name="slide_project",
    )(idx, cache, gain, weight)


def depth_of(x):
    return sum(((x & mask) == 0).astype(jnp.int32) for mask in (1, 3, 7, 15))


def attend_kernel(
    idx, *refs
):
    sources, (o0, o1, o2, o3), targets = refs[:5], refs[5:9], refs[9:14]
    q, peak, total, acc, sems = refs[14:]
    emb, q_cache, mine, theirs, out_w = targets
    loads = [
        pltpu.make_async_copy(source, target, sems.at[i])
        for i, (source, target) in enumerate(zip(sources, targets))
    ]
    for load in loads:
        load.start()
    mp, seq = idx[0], idx[1]
    first_head = mp * 4
    hw = q_cache.shape[1]
    scale = HDL ** (-0.5)
    slots = emb.shape[0]
    loads[0].wait()
    loads[1].wait()
    tail = emb[:, 3 * hw :]
    col = iota((8, tail.shape[1]), 1)
    digits = jnp.where(col == 0, 64.0, jnp.where(col == 1, 1.0, 0.0)).astype(BF)
    pos = dot_t(digits, tail).astype(jnp.int32)[0:1]
    spread = dot_t(tail, digits).astype(jnp.int32)[:, 0:1]
    own = seq * ROWS + local_row(iota((ROWS, 1), 0), 0, 0)
    match = own == pos
    found = jnp.max(match.astype(jnp.int32), axis=1, keepdims=True) > 0
    placed = dot(match.astype(BF), emb[:, 2 * hw : 3 * hw])
    q[...] = jnp.where(found, placed, q_cache[...])

    def head_mask(n, h):
        column = iota((n, hw), 1)
        return (column >= h * HDL) & (column < (h + 1) * HDL)

    def queries(level):
        n = ROWS >> level
        got = []
        for h in range(4):
            rows = q[...] if level == 0 else q[pl.ds(pick_start(first_head + h, level), n), :]
            got.append(jnp.where(head_mask(n, h), rows, 0.0))
        return jnp.concatenate(got, axis=0).astype(BF)

    full_q = queries(0)
    s = dot_t(full_q, emb[:, 0:hw]) * scale
    cross = (pos ^ (seq * ROWS)) >> 9
    first = sum(((cross >> b) != 0).astype(jnp.int32) for b in range(4))
    times = []
    for h in range(4):
        q_depth = depth_of(own ^ (first_head + h))
        k_depth = jnp.where(pos < 0, -1, depth_of(pos ^ (first_head + h)) - first)
        times.append(jnp.maximum(jnp.minimum(k_depth, q_depth - first) + 1, 0))
    times = jnp.concatenate(times, axis=0).astype(F32)
    s = jnp.where(times > 0.0, s, FLOOR_SCORE)
    m = jnp.max(s, axis=-1, keepdims=True)
    e = times * jnp.exp(s - m)
    peak[...] = jnp.broadcast_to(m, peak.shape)
    total[...] = jnp.broadcast_to(jnp.sum(e, axis=-1, keepdims=True), total.shape)
    acc[...] = dot(e.astype(BF), emb[:, hw : 2 * hw])

    loads[2].wait()
    loads[3].wait()
    for level in range(BRANCHES):
        n = ROWS >> level
        qb = full_q if level == 0 else queries(level)
        half = 512 if level == BRANCHES - 1 else 256
        low = BASES[level]
        last = level == BRANCHES - 1
        pitch = 16 if last else n
        turned = (rev4(spread & 15) << 3) + ((spread & 127) >> 4)
        cross_rows = (spread >> 7) ^ seq
        key = (cross_rows & 1) * half + (cross_rows >> 1) * pitch + (turned & (n - 1))
        inside = jnp.where((pos >= 0) & (first <= level), 1, 0)
        head_row = first_head + iota((8, slots), 0)
        hits = (((pos ^ head_row) & ((1 << level) - 1)) == 0) & (inside > 0)
        key_lane = iota((slots, 2 * half), 1)
        bias = dot(
            jnp.where(hits, FLOOR_SCORE, 0.0).astype(BF), (key_lane == key).astype(BF)
        )
        if last:
            bias = jnp.where((iota((8, 2 * half), 1) & 15) >= 8, FLOOR_SCORE, bias)
        sides = []
        for number, side in enumerate((mine, theirs)):
            s = dot_t(qb, side[low : low + half, 0:hw]) * scale
            flags = bias[0:4, number * half : (number + 1) * half]
            s = s.reshape(4, n, half) + flags[:, None, :]
            sides.append(s.reshape(4 * n, half))
        m = jnp.maximum(
            jnp.max(sides[0], axis=-1, keepdims=True), jnp.max(sides[1], axis=-1, keepdims=True)
        )
        e0, e1 = jnp.exp(sides[0] - m), jnp.exp(sides[1] - m)
        t = jnp.sum(e0, axis=-1, keepdims=True) + jnp.sum(e1, axis=-1, keepdims=True)
        o = dot(e0.astype(BF), mine[low : low + half, hw : 2 * hw]) + dot(
            e1.astype(BF), theirs[low : low + half, hw : 2 * hw]
        )
        for h in range(4):
            start = h * ROWS + (0 if level == 0 else pick_start(first_head + h, level))
            at = pl.ds(pl.multiple_of(start, 8), n)
            part = slice(h * n, (h + 1) * n)
            before = peak[at, :]
            after = jnp.maximum(before, m[part])
            keep, add = jnp.exp(before - after), jnp.exp(m[part] - after)
            peak[at, :] = after
            total[at, :] = total[at, :] * keep + t[part] * add
            acc[at, :] = acc[at, :] * keep[:, 0:1] + o[part] * add[:, 0:1]

    attended = jnp.zeros((ROWS, hw), F32)
    for h in range(4):
        rows = slice(h * ROWS, (h + 1) * ROWS)
        attended = jnp.where(head_mask(ROWS, h), acc[rows, :] / total[rows, 0:1], attended)
    turn = (local_row(iota((ROWS, ROWS), 1), 0, 0) == iota((ROWS, ROWS), 0)).astype(BF)
    attended = dot(turn, attended.astype(BF)).astype(BF)
    loads[4].wait()
    for d, o in enumerate((o0, o1, o2, o3)):
        o[...] = dot(attended, out_w[lax.rem(mp + d, 4)]).astype(BF)


def attend(idx, q_cache, mine, theirs, emb, out_w):
    hw = q_cache.shape[1]
    return pl.pallas_call(
        attend_kernel,
        out_shape=(jax.ShapeDtypeStruct((ROWS, hw), BF),) * 4,
        in_specs=[whole(pltpu.SMEM)] + [whole(pltpu.HBM)] * 5,
        out_specs=(whole(),) * 4,
        scratch_shapes=[pltpu.VMEM(x.shape, x.dtype) for x in (emb, q_cache, mine, theirs, out_w)]
        + [
            pltpu.VMEM((ROWS, hw), F32),
            pltpu.VMEM((4 * ROWS, 128), F32),
            pltpu.VMEM((4 * ROWS, 128), F32),
            pltpu.VMEM((4 * ROWS, hw), F32),
            pltpu.SemaphoreType.DMA((5,)),
        ],
        compiler_params=params(60),
        name="attend",
    )(idx, emb, q_cache, mine, theirs, out_w)


def shift_mp(x, k):
    return lax.ppermute(x, "mp", [(i, (i + k) % 4) for i in range(4)])


def swap_seq(x, bit):
    return lax.ppermute(x, "seq", [(i, i ^ bit) for i in range(64)])


def local(
    tile_batch,
    positions,
    counts,
    vit_gain,
    vit_qkv,
    vit_out,
    tile_proj,
    seq_cache,
    long_gain,
    long_qkv,
    long_out,
):
    mp, seq = lax.axis_index("mp"), lax.axis_index("seq")
    idx = jnp.concatenate([jnp.stack([mp, seq]).astype(jnp.int32), counts, positions])
    slots, _, width = tile_batch.shape
    model = seq_cache.shape[1]
    hw = long_qkv.shape[-1]

    left, right = shift_mp(tile_batch, 1), shift_mp(tile_batch, 3)
    tile_w = vit_qkv.transpose(1, 0, 2)
    gain = vit_gain.reshape(1, 4 * width)

    slide_w = long_qkv.transpose(1, 2, 0).reshape(3 * hw, model)
    gain_row = long_gain.reshape(1, model)
    q_cache, picks = slide_project(idx, seq_cache, gain_row, slide_w)
    proj_here = lax.dynamic_slice_in_dim(tile_proj, mp * width, width, 0)
    joined = jnp.concatenate([dot(vit_out, tile_proj).astype(BF), proj_here], axis=0)
    far = [shift_mp(left[0:2], 1), shift_mp(right[2:4], 3)]

    kept = []

    def step(have, level):
        have = jnp.concatenate([have, swap_seq(have, 2 << level)], axis=0)
        n = ROWS >> level
        kept.append(have[:, 0:n].reshape(-1, 2 * hw))
        return have[:, n:]

    have = step(step(picks[None], 0), 1)
    far[0], have, joined = lax.optimization_barrier((far[0], have, joined))
    first = encode(idx, 0, tile_batch, left, right, far[0], gain, tile_w)
    have = step(have, 2)
    far[1], first = lax.optimization_barrier((far[1], first))
    second = encode(idx, 1, tile_batch, left, right, far[1], gain, tile_w)
    first, second, have = lax.optimization_barrier((first, second, have))
    partial = dot(jnp.concatenate([first, second], axis=0).astype(BF), joined)
    shares = [partial] + [shift_mp(partial, k) for k in (1, 3, 2)]
    last = have[:, 16:]
    across = [swap_seq(have, 16), swap_seq(last, 32), swap_seq(last, 48)]
    shares, across = lax.optimization_barrier((shares, across))
    kept += [x[:, 0:16].reshape(-1, 2 * hw) for x in (have, across[0])]
    kept += [x.reshape(-1, 2 * hw) for x in (last, across[0][:, 16:], across[1], across[2])]
    mine = jnp.concatenate(kept, axis=0)
    theirs = swap_seq(mine, 1)
    emb = embed_rows(idx, shares, gain_row, slide_w)
    emb = lax.all_to_all(jnp.broadcast_to(emb[None], (64,) + emb.shape), "seq", 0, 0)
    emb = emb.reshape(64 * slots, emb.shape[2])

    out_w = long_out.reshape(hw, 4, hw).transpose(1, 0, 2)
    o0, o1, o2, o3 = attend(idx, q_cache, mine, theirs, emb, out_w)
    terms = [o0, shift_mp(o1, 1), shift_mp(o2, 2), shift_mp(o3, 3)]
    a, b, c, d = [term.astype(F32) for term in terms]
    return ((a + b) + (c + d)).astype(BF)


def solution(mesh):
    placed = (
        P("seq", None, "mp"),
        P("seq"),
        P("seq"),
        P(),
        P(None, None, "mp"),
        P("mp", None),
        P(),
        P("seq", None),
        P(),
        P(None, None, "mp"),
        P("mp", None),
    )
    return jax.shard_map(
        local, mesh=mesh, in_specs=placed, out_specs=P("seq", "mp"), check_vma=False
    )
```

```python
import functools
import math

import jax
import jax.numpy as jnp
from jax import lax
from jax.experimental import pallas as pl
from jax.experimental.pallas import tpu as pltpu
from jax.sharding import PartitionSpec as P

HDT = 64
HDL = 48
BRANCHES = 5
EPSILON = 1e-05
FLOOR_SCORE = -1e30
BF = jnp.bfloat16
F32 = jnp.float32
ROWS = 128
BASES = (0, 256, 512, 768, 1024)


def params(mib=40):
    return pltpu.CompilerParams(vmem_limit_bytes=mib * 2**20)


def whole(kind=pltpu.VMEM):
    return pl.BlockSpec(memory_space=kind)


def dot(a, b):
    return jnp.dot(a, b, preferred_element_type=F32)


def dot_t(a, b):
    return lax.dot_general(a, b, (((1,), (1,)), ((), ())), preferred_element_type=F32)


def iota(shape, dim):
    return lax.broadcasted_iota(jnp.int32, shape, dim)


def encode_kernel(idx, own, left, right, far, gain, weight, out, xn, qk):
    mp = idx[0]
    tokens, width = own.shape[1], own.shape[2]
    unit = HDT ** (-0.5) * math.log2(math.e)
    features = 4 * width
    starts = [pl.multiple_of(lax.rem(mp + shift, 4) * width, 128) for shift in (0, 3, 1, 2)]
    for t in range(2):
        parts = [own[t], left[t], right[t], far[t]]
        wide = [part.astype(F32) for part in parts]
        total = sum(jnp.sum(part, axis=-1, keepdims=True) for part in wide)
        mean = total * (1.0 / features)
        centred = [part - mean for part in wide]
        spread = sum(jnp.sum(part * part, axis=-1, keepdims=True) for part in centred)
        scale = lax.rsqrt(spread * (1.0 / features) + EPSILON)
        for d in range(4):
            columns = pl.ds(starts[d], width)
            xn[t * tokens : (t + 1) * tokens, columns] = (
                centred[d] * scale * gain[:, columns]
            ).astype(BF)
        out[t : t + 1, width : 2 * width] = jnp.sum(wide[0], axis=0, keepdims=True) * (1.0 / tokens)
    for part in range(2):
        qk[:, part * width : (part + 1) * width] = dot(xn[...], weight[part]).astype(BF)
    lane = iota((tokens, 2 * HDT), 1)
    pooled = []
    for t in range(2):
        low, high = t * tokens, (t + 1) * tokens
        rows = []
        for pair in range(width // (2 * HDT)):
            q2 = qk[low:high, pair * 128 : (pair + 1) * 128]
            k2 = qk[low:high, width + pair * 128 : width + (pair + 1) * 128]
            for half in range(2):
                qm = jnp.where((lane >= HDT) == (half == 1), q2, jnp.zeros((), BF))
                s = dot_t(qm, k2)
                e = jnp.exp2((s - jnp.max(s, axis=-1, keepdims=True)) * unit)
                share = 1.0 / (jnp.sum(e, axis=-1, keepdims=True) * tokens)
                rows.append(jnp.sum(e * share, axis=0, keepdims=True))
        rows.append(jnp.zeros((8 - len(rows), tokens), F32))
        mix = jnp.concatenate(rows, axis=0).astype(BF)
        pooled.append(dot(mix, xn[low:high, :]))
    acc = dot(jnp.concatenate(pooled, axis=0).astype(BF), weight[2])
    keep = (iota((16, width), 0) & 7) == (iota((16, width), 1) >> 6)
    acc = jnp.where(keep, acc, 0.0)
    for t in range(2):
        out[t : t + 1, 0:width] = jnp.sum(acc[t * 8 : (t + 1) * 8], axis=0, keepdims=True)


def encode(idx, chunk, own, left, right, far, gain, weight):
    tokens, width = own.shape[1], own.shape[2]
    block = pl.BlockSpec((2, tokens, width), lambda i: (chunk, 0, 0))
    far_block = pl.BlockSpec((2, tokens, width), lambda i: (0, 0, 0))
    return pl.pallas_call(
        encode_kernel,
        grid=(1,),
        out_shape=jax.ShapeDtypeStruct((2, 2 * width), F32),
        in_specs=[whole(pltpu.SMEM), block, block, block, far_block, whole(), whole()],
        out_specs=whole(),
        scratch_shapes=[
            pltpu.VMEM((2 * tokens, 4 * width), BF),
            pltpu.VMEM((2 * tokens, 2 * width), BF),
        ],
        compiler_params=params(20),
        cost_estimate=pl.CostEstimate(
            flops=6 * 10**9, bytes_accessed=8 * 10**6, transcendentals=8 * 10**5
        ),
        name="encode",
    )(idx, own, left, right, far, gain, weight)


def norm_rows(x, gain):
    mean = jnp.mean(x, axis=-1, keepdims=True)
    centre = x - mean
    spread = jnp.mean(centre * centre, axis=-1, keepdims=True)
    return (centre * lax.rsqrt(spread + EPSILON) * gain).astype(BF)


def slot_digits(idx, slot):
    place = jnp.where(slot < idx[2], idx[3 + slot], -64)
    return (place >> 6).astype(F32), (place & 63).astype(F32)


def embed_kernel(idx, a, b, c, d, gain, weight, out):
    width = weight.shape[0]
    third = width // 3
    total = (a[...] + b[...]) + (c[...] + d[...])
    normed = norm_rows(total.astype(BF).astype(F32), gain[...])
    out[:, 0 : 2 * third] = dot_t(normed, weight[third:, :]).astype(BF)
    out[:, 2 * third : width] = dot_t(normed, weight[0:third, :]).astype(BF)
    shape = (out.shape[0], out.shape[1] - width)
    row, column = iota(shape, 0), iota(shape, 1)
    tail = jnp.zeros(shape, F32)
    for slot in range(shape[0]):
        high, low = slot_digits(idx, slot)
        tail = jnp.where((row == slot) & (column == 0), high, tail)
        tail = jnp.where((row == slot) & (column == 1), low, tail)
    out[:, width:] = tail.astype(BF)


def embed_rows(idx, parts, gain, weight):
    rows, width = parts[0].shape[0], weight.shape[0]
    return pl.pallas_call(
        embed_kernel,
        out_shape=jax.ShapeDtypeStruct((rows, width + 64), BF),
        in_specs=[whole(pltpu.SMEM)] + [whole()] * 6,
        out_specs=whole(),
        compiler_params=params(20),
        name="embed_rows",
    )(idx, *parts, gain, weight)


def rev4(x):
    return ((x & 1) << 3) | ((x & 2) << 1) | ((x & 4) >> 1) | ((x & 8) >> 3)


def pick_start(head, level):
    return pl.multiple_of((rev4(head & 15) >> (4 - level)) * (ROWS >> level), 8)


def local_row(j, level, head):
    bits = j >> 3
    free = 4 - level
    turned = rev4(bits) >> (4 - free) if free else bits * 0
    return (j & 7) * 16 + (turned << level) + (head & ((1 << level) - 1))


def slide_kernel(idx, cache, gain, weight, q_out, picks, kv):
    heads_width = q_out.shape[1]
    first_head = idx[0] * 4
    row = iota((ROWS, ROWS), 0)
    turn = (local_row(row, 0, 0) == iota((ROWS, ROWS), 1)).astype(BF)
    normed = norm_rows(cache[...].astype(F32), gain[...])
    normed = dot(turn, normed).astype(BF)
    q_out[...] = dot_t(normed, weight[0:heads_width, :]).astype(BF).astype(F32)
    kv[...] = dot_t(normed, weight[heads_width:, :]).astype(BF).astype(F32)
    base = 0
    for level in range(BRANCHES):
        n = ROWS >> level
        column = iota((n, 2 * heads_width), 1)
        column = jnp.where(column >= heads_width, column - heads_width, column)
        got = jnp.zeros((n, 2 * heads_width), F32)
        for h in range(4):
            here = (column >= h * HDL) & (column < (h + 1) * HDL)
            got = jnp.where(here, kv[pl.ds(pick_start(first_head + h, level), n), :], got)
        if level == BRANCHES - 1:
            got = jnp.concatenate([got, jnp.zeros((8, 2 * heads_width), F32)], axis=0)
        picks[base : base + got.shape[0], :] = got.astype(BF)
        base += n


def slide_project(idx, cache, gain, weight):
    hw = weight.shape[0] // 3
    return pl.pallas_call(
        slide_kernel,
        out_shape=(
            jax.ShapeDtypeStruct((ROWS, hw), F32),
            jax.ShapeDtypeStruct((2 * ROWS, 2 * hw), BF),
        ),
        in_specs=[whole(pltpu.SMEM)] + [whole()] * 3,
        out_specs=(whole(),) * 2,
        scratch_shapes=[pltpu.VMEM((ROWS, 2 * hw), F32)],
        compiler_params=params(20),
        name="slide_project",
    )(idx, cache, gain, weight)


def depth_of(x):
    return sum(((x & mask) == 0).astype(jnp.int32) for mask in (1, 3, 7, 15))


def attend_kernel(
    idx, *refs
):
    sources, (o0, o1, o2, o3), targets = refs[:5], refs[5:9], refs[9:14]
    q, peak, total, acc, sems = refs[14:]
    emb, q_cache, mine, theirs, out_w = targets
    loads = [
        pltpu.make_async_copy(source, target, sems.at[i])
        for i, (source, target) in enumerate(zip(sources, targets))
    ]
    for load in loads:
        load.start()
    mp, seq = idx[0], idx[1]
    first_head = mp * 4
    hw = q_cache.shape[1]
    scale = HDL ** (-0.5)
    slots = emb.shape[0]
    loads[0].wait()
    loads[1].wait()
    tail = emb[:, 3 * hw :]
    col = iota((8, tail.shape[1]), 1)
    digits = jnp.where(col == 0, 64.0, jnp.where(col == 1, 1.0, 0.0)).astype(BF)
    pos = dot_t(digits, tail).astype(jnp.int32)[0:1]
    spread = dot_t(tail, digits).astype(jnp.int32)[:, 0:1]
    own = seq * ROWS + local_row(iota((ROWS, 1), 0), 0, 0)
    match = own == pos
    found = jnp.max(match.astype(jnp.int32), axis=1, keepdims=True) > 0
    placed = dot(match.astype(BF), emb[:, 2 * hw : 3 * hw])
    q[...] = jnp.where(found, placed, q_cache[...])

    def head_mask(n, h):
        column = iota((n, hw), 1)
        return (column >= h * HDL) & (column < (h + 1) * HDL)

    def queries(level):
        n = ROWS >> level
        got = []
        for h in range(4):
            rows = q[...] if level == 0 else q[pl.ds(pick_start(first_head + h, level), n), :]
            got.append(jnp.where(head_mask(n, h), rows, 0.0))
        return jnp.concatenate(got, axis=0).astype(BF)

    full_q = queries(0)
    s = dot_t(full_q, emb[:, 0:hw]) * scale
    cross = (pos ^ (seq * ROWS)) >> 9
    first = sum(((cross >> b) != 0).astype(jnp.int32) for b in range(4))
    times = []
    for h in range(4):
        q_depth = depth_of(own ^ (first_head + h))
        k_depth = jnp.where(pos < 0, -1, depth_of(pos ^ (first_head + h)) - first)
        times.append(jnp.maximum(jnp.minimum(k_depth, q_depth - first) + 1, 0))
    times = jnp.concatenate(times, axis=0).astype(F32)
    s = jnp.where(times > 0.0, s, FLOOR_SCORE)
    m = jnp.max(s, axis=-1, keepdims=True)
    e = times * jnp.exp(s - m)
    peak[...] = jnp.broadcast_to(m, peak.shape)
    total[...] = jnp.broadcast_to(jnp.sum(e, axis=-1, keepdims=True), total.shape)
    acc[...] = dot(e.astype(BF), emb[:, hw : 2 * hw])

    loads[2].wait()
    loads[3].wait()
    for level in range(BRANCHES):
        n = ROWS >> level
        qb = full_q if level == 0 else queries(level)
        half = 512 if level == BRANCHES - 1 else 256
        low = BASES[level]
        last = level == BRANCHES - 1
        pitch = 16 if last else n
        turned = (rev4(spread & 15) << 3) + ((spread & 127) >> 4)
        cross_rows = (spread >> 7) ^ seq
        key = (cross_rows & 1) * half + (cross_rows >> 1) * pitch + (turned & (n - 1))
        inside = jnp.where((pos >= 0) & (first <= level), 1, 0)
        head_row = first_head + iota((8, slots), 0)
        hits = (((pos ^ head_row) & ((1 << level) - 1)) == 0) & (inside > 0)
        key_lane = iota((slots, 2 * half), 1)
        bias = dot(
            jnp.where(hits, FLOOR_SCORE, 0.0).astype(BF), (key_lane == key).astype(BF)
        )
        if last:
            bias = jnp.where((iota((8, 2 * half), 1) & 15) >= 8, FLOOR_SCORE, bias)
        sides = []
        for number, side in enumerate((mine, theirs)):
            s = dot_t(qb, side[low : low + half, 0:hw]) * scale
            flags = bias[0:4, number * half : (number + 1) * half]
            s = s.reshape(4, n, half) + flags[:, None, :]
            sides.append(s.reshape(4 * n, half))
        m = jnp.maximum(
            jnp.max(sides[0], axis=-1, keepdims=True), jnp.max(sides[1], axis=-1, keepdims=True)
        )
        e0, e1 = jnp.exp(sides[0] - m), jnp.exp(sides[1] - m)
        t = jnp.sum(e0, axis=-1, keepdims=True) + jnp.sum(e1, axis=-1, keepdims=True)
        o = dot(e0.astype(BF), mine[low : low + half, hw : 2 * hw]) + dot(
            e1.astype(BF), theirs[low : low + half, hw : 2 * hw]
        )
        for h in range(4):
            start = h * ROWS + (0 if level == 0 else pick_start(first_head + h, level))
            at = pl.ds(pl.multiple_of(start, 8), n)
            part = slice(h * n, (h + 1) * n)
            before = peak[at, :]
            after = jnp.maximum(before, m[part])
            keep, add = jnp.exp(before - after), jnp.exp(m[part] - after)
            peak[at, :] = after
            total[at, :] = total[at, :] * keep + t[part] * add
            acc[at, :] = acc[at, :] * keep[:, 0:1] + o[part] * add[:, 0:1]

    attended = jnp.zeros((ROWS, hw), F32)
    for h in range(4):
        rows = slice(h * ROWS, (h + 1) * ROWS)
        attended = jnp.where(head_mask(ROWS, h), acc[rows, :] / total[rows, 0:1], attended)
    turn = (local_row(iota((ROWS, ROWS), 1), 0, 0) == iota((ROWS, ROWS), 0)).astype(BF)
    attended = dot(turn, attended.astype(BF)).astype(BF)
    loads[4].wait()
    for d, o in enumerate((o0, o1, o2, o3)):
        o[...] = dot(attended, out_w[lax.rem(mp + d, 4)]).astype(BF)


def attend(idx, q_cache, mine, theirs, emb, out_w):
    hw = q_cache.shape[1]
    return pl.pallas_call(
        attend_kernel,
        out_shape=(jax.ShapeDtypeStruct((ROWS, hw), BF),) * 4,
        in_specs=[whole(pltpu.SMEM)] + [whole(pltpu.HBM)] * 5,
        out_specs=(whole(),) * 4,
        scratch_shapes=[pltpu.VMEM(x.shape, x.dtype) for x in (emb, q_cache, mine, theirs, out_w)]
        + [
            pltpu.VMEM((ROWS, hw), F32),
            pltpu.VMEM((4 * ROWS, 128), F32),
            pltpu.VMEM((4 * ROWS, 128), F32),
            pltpu.VMEM((4 * ROWS, hw), F32),
            pltpu.SemaphoreType.DMA((5,)),
        ],
        compiler_params=params(60),
        name="attend",
    )(idx, emb, q_cache, mine, theirs, out_w)


def shift_mp(x, k):
    return lax.ppermute(x, "mp", [(i, (i + k) % 4) for i in range(4)])


def swap_seq(x, bit):
    return lax.ppermute(x, "seq", [(i, i ^ bit) for i in range(64)])


def local(
    tile_batch,
    positions,
    counts,
    vit_gain,
    vit_qkv,
    vit_out,
    tile_proj,
    seq_cache,
    long_gain,
    long_qkv,
    long_out,
):
    mp, seq = lax.axis_index("mp"), lax.axis_index("seq")
    idx = jnp.concatenate([jnp.stack([mp, seq]).astype(jnp.int32), counts, positions])
    slots, _, width = tile_batch.shape
    model = seq_cache.shape[1]
    hw = long_qkv.shape[-1]

    left, right = shift_mp(tile_batch, 1), shift_mp(tile_batch, 3)
    tile_w = vit_qkv.transpose(1, 0, 2)
    gain = vit_gain.reshape(1, 4 * width)

    slide_w = long_qkv.transpose(1, 2, 0).reshape(3 * hw, model)
    gain_row = long_gain.reshape(1, model)
    q_cache, picks = slide_project(idx, seq_cache, gain_row, slide_w)
    proj_here = lax.dynamic_slice_in_dim(tile_proj, mp * width, width, 0)
    joined = jnp.concatenate([dot(vit_out, tile_proj).astype(BF), proj_here], axis=0)
    far = [shift_mp(left[0:2], 1), shift_mp(right[2:4], 3)]

    kept = []

    def step(have, level):
        have = jnp.concatenate([have, swap_seq(have, 2 << level)], axis=0)
        if level == BRANCHES - 1:
            return have
        n = ROWS >> level
        kept.append(have[:, 0:n].reshape(-1, 2 * hw))
        return have[:, n:]

    have = step(step(picks[None], 0), 1)
    far[0], have, joined = lax.optimization_barrier((far[0], have, joined))
    first = encode(idx, 0, tile_batch, left, right, far[0], gain, tile_w)
    have = step(have, 2)
    far[1], have, first = lax.optimization_barrier((far[1], have, first))
    second = encode(idx, 1, tile_batch, left, right, far[1], gain, tile_w)
    have = step(have, 3)
    first, second, have = lax.optimization_barrier((first, second, have))
    partial = dot(jnp.concatenate([first, second], axis=0).astype(BF), joined)
    shares = [partial] + [shift_mp(partial, k) for k in (1, 3, 2)]
    have = step(have, 4)
    mine = jnp.concatenate(kept + [have.reshape(-1, 2 * hw)], axis=0)
    shares, mine = lax.optimization_barrier((shares, mine))
    theirs = swap_seq(mine, 1)
    emb = embed_rows(idx, shares, gain_row, slide_w)
    emb = lax.all_to_all(jnp.broadcast_to(emb[None], (64,) + emb.shape), "seq", 0, 0)
    emb = emb.reshape(64 * slots, emb.shape[2])

    out_w = long_out.reshape(hw, 4, hw).transpose(1, 0, 2)
    o0, o1, o2, o3 = attend(idx, q_cache, mine, theirs, emb, out_w)
    terms = [o0, shift_mp(o1, 1), shift_mp(o2, 2), shift_mp(o3, 3)]
    a, b, c, d = [term.astype(F32) for term in terms]
    return ((a + b) + (c + d)).astype(BF)


def solution(mesh):
    placed = (
        P("seq", None, "mp"),
        P("seq"),
        P("seq"),
        P(),
        P(None, None, "mp"),
        P("mp", None),
        P(),
        P("seq", None),
        P(),
        P(None, None, "mp"),
        P("mp", None),
    )
    return jax.shard_map(
        local, mesh=mesh, in_specs=placed, out_specs=P("seq", "mp"), check_vma=False
    )
```
